256 devices in a mesh: slab: 64 (over z, x, core), chan: 4 (over y).
Axes of the slice: x: 4, y: 4, z: 8, core: 2. Of those that a mesh axis runs over, the one named last changes fastest.
Arguments:
- point_feats: bfloat16 [32, 65536], P(None, 'slab'), may hold values from -6 to 6
- cell_coords: int32 [3, 65536], P(None, 'slab'), may hold values from 0 to 2047, as said below
- send_counts: int32 [64, 64], P('slab'), may hold values from 1 to 16, as said below
- lift_weight: bfloat16 [32, 32], P(None, 'chan'), may hold values from -1 to 1
- spec_weight: float32 [2, 32, 32, 64, 64, 32], P(None, None, 'chan', 'slab'), may hold values from -3 to 3
- skip_weight: bfloat16 [32, 32], P(None, 'chan'), may hold values from -1 to 1
- spec_bias: float32 [32], P('chan'), may hold values from -3 to 3
- out_weight: bfloat16 [32, 4], P('chan'), may hold values from -1 to 1
- out_bias: float32 [4], replicated, may hold values from -4 to 4
Outputs:
- surface_fields: float32 [4, 65536], P(None, 'slab')
The draws below stay inside these ranges and needn't reach their ends.
Inputs may be any that keep to these rules, and one draw needn't show every extreme that they name: `cell_coords`: the slot s * 1024 + d * 16 + j lies in slab d: its first coordinate // 32 equals d. `send_counts`: each entry counts the live slots of patch s for slab d; in every draw some slab receives 16 live points from every patch.
All inputs are finite; a program needn't handle non-finite values.
Results may differ from the reference program's by a relative error of at most 0.0013.
Values may be sent and summed in bfloat16 or wider, within the bound.
A program may use at most 192 MiB of HBM per device.

```python
import jax
import jax.numpy as jnp
from jax import lax

GRID = 128
C = 32
MZ = 32
F_IN = 32
NOUT = 4
SUB = 16
SLABS = 64
CAP = 16
POINTS = 65536
XP = 2
KY = 64
KX = 64


def draw_send_counts(key, part):
    key = jax.random.fold_in(key, 11)
    first_key, second_key, column_key = jax.random.split(key, 3)
    first = jax.random.randint(first_key, (SLABS, SLABS), 1, CAP + 1)
    second = jax.random.randint(second_key, (SLABS, SLABS), 1, CAP + 1)
    busiest = jax.random.randint(column_key, (), 0, SLABS)
    columns = jnp.arange(SLABS)[None, :]
    return jnp.where(columns == busiest, CAP, jnp.minimum(first, second)).astype(jnp.int32)


def draw_cell_coords(key, part):
    key = jax.random.fold_in(key, 23)
    first_key, rest_key = jax.random.split(key, 2)
    target = jnp.arange(POINTS) // CAP % SLABS
    offsets = jax.random.randint(first_key, (POINTS,), 0, XP * SUB)
    first = target * (XP * SUB) + offsets
    others = jax.random.randint(rest_key, (2, POINTS), 0, GRID * SUB)
    return jnp.concatenate([first[None, :], others], axis=0).astype(jnp.int32)


def shard_levels(stream_key, dims, pieces, smallest, top_value):
    factor_of, own = 1.0, jax.random.fold_in(stream_key, 6)
    for position, blocks in pieces:
        draws = jnp.exp(jax.random.uniform(jax.random.fold_in(own, position), (blocks,), jnp.float32, smallest / len(pieces), top_value / len(pieces)))
        factor_of = factor_of * jnp.repeat(draws, dims[position] // blocks).reshape([-1 if axis == position else 1 for axis in range(len(dims))])
    return factor_of


def bell_draw(stream_key, extent, scale, bound, cuts=(), kind=jnp.bfloat16):
    factor_of = shard_levels(stream_key, extent, cuts, -0.22, 0.18) if cuts else 1.0
    drawn = jax.random.normal(stream_key, extent, jnp.float32) * scale * factor_of
    return jnp.minimum(jnp.maximum(drawn, -bound), bound).astype(kind)


def setup_inputs(seed: int = 0) -> dict:
    keys = jax.random.split(jax.random.key(seed), 10)
    return {
        "point_feats": bell_draw(keys[0], (F_IN, POINTS), 1.0, 6.0, ((1, 64),)),
        "cell_coords": draw_cell_coords(jax.random.fold_in(keys[9], 71), 0),
        "send_counts": draw_send_counts(jax.random.fold_in(keys[9], 71), 0),
        "lift_weight": bell_draw(keys[3], (F_IN, C), F_IN ** -0.5, 1.0, ((1, 4),)),
        "spec_weight": bell_draw(keys[4], (2, C, C, KY, KX, MZ), 0.5, 3.0, ((2, 4), (3, 64)), jnp.float32),
        "skip_weight": bell_draw(keys[5], (C, C), C ** -0.5, 1.0, ((1, 4),)),
        "spec_bias": bell_draw(keys[6], (C,), 0.5, 3.0, ((0, 4),), jnp.float32),
        "out_weight": bell_draw(keys[7], (C, NOUT), C ** -0.5, 1.0, ((0, 4),)),
        "out_bias": bell_draw(keys[8], (NOUT,), 1.0, 4.0, (), jnp.float32),
    }


def kept_modes():
    return jnp.concatenate([jnp.arange(MZ), jnp.arange(GRID - MZ, GRID)]).astype(jnp.int32)


def stencil(coords):
    cells = coords // SUB
    frac = ((coords % SUB).astype(jnp.float32) + 0.5) / SUB
    side = GRID + 1
    indices = []
    weights = []
    for dx in (0, 1):
        for dy in (0, 1):
            for dz in (0, 1):
                flat = ((cells[0] + dx) * side + cells[1] + dy) * side + cells[2] + dz
                wx = frac[0] if dx else 1.0 - frac[0]
                wy = frac[1] if dy else 1.0 - frac[1]
                wz = frac[2] if dz else 1.0 - frac[2]
                indices.append(flat.astype(jnp.int32))
                weights.append(wx * wy * wz)
    return jnp.stack(indices), jnp.stack(weights)


def spectral_layer(latent32, spec_weight):
    vhat = jnp.fft.rfftn(latent32, axes=(1, 2, 3))
    modes = kept_modes()
    chosen = vhat[:, modes][:, :, modes][..., :MZ]
    wcomplex = spec_weight[0] + 1j * spec_weight[1]
    mixed = jnp.einsum('ioyxm,ixym->oxym', wcomplex, chosen)
    full = jnp.zeros((C, GRID, GRID, GRID // 2 + 1), dtype=vhat.dtype)
    full = full.at[:, modes[:, None], modes[None, :], :MZ].set(mixed)
    return jnp.fft.irfftn(full, s=(GRID, GRID, GRID), axes=(1, 2, 3))


def reference(point_feats, cell_coords, send_counts, lift_weight, spec_weight, skip_weight, spec_bias, out_weight, out_bias):
    live = (jnp.arange(CAP)[None, None, :] < send_counts[:, :, None]).reshape(-1)
    embed = jnp.dot(lift_weight.T, point_feats, preferred_element_type=jnp.float32)
    embed = jnp.where(live[None], embed, 0.0).astype(jnp.bfloat16)
    indices, weights = stencil(cell_coords)
    side = GRID + 1
    accum = jnp.zeros((C, side * side * side), jnp.float32)
    embed32 = embed.astype(jnp.float32)
    for corner in range(8):
        accum = accum.at[:, indices[corner]].add(weights[corner][None] * embed32)
    latent = accum.reshape(C, side, side, side)[:, :GRID, :GRID, :GRID].astype(jnp.bfloat16)
    latent32 = latent.astype(jnp.float32)
    spectral = spectral_layer(latent32, spec_weight)
    skipped = jnp.einsum('io,ixyz->oxyz', skip_weight.astype(jnp.float32), latent32)
    hidden = jax.nn.gelu(spectral + skipped + spec_bias[:, None, None, None]).astype(jnp.bfloat16)
    padded = jnp.pad(hidden, ((0, 0), (0, 1), (0, 1), (0, 1))).reshape(C, -1)
    samples = jnp.zeros((C, cell_coords.shape[1]), jnp.float32)
    for corner in range(8):
        samples = samples + padded[:, indices[corner]].astype(jnp.float32) * weights[corner][None]
    heads = jnp.dot(out_weight.T.astype(jnp.float32), samples, precision=lax.Precision.HIGHEST)
    return jnp.where(live[None], heads + out_bias[:, None], 0.0)
```

```python
import functools
import math

import jax
import jax.numpy as jnp
import numpy as np
from jax import lax
from jax.experimental import pallas as pl
from jax.experimental.pallas import tpu as pltpu
from jax.sharding import PartitionSpec as P

GRID = 128
MZ = 32
CAP = 16
SLABS = 64
CHANS = 4
POINTS = 1024
MODES = np.concatenate([np.arange(MZ), np.arange(GRID - MZ, GRID)])
MESH = pl.DeviceIdType.MESH
F32 = jnp.float32
BF16 = jnp.bfloat16


def wave(freqs, positions):
    angle = (freqs[:, None] * positions[None, :] % GRID) * (2.0 * math.pi / GRID)
    return np.cos(angle), np.sin(angle)


def tables():
    spots = np.arange(GRID)
    cos_y, sin_y = wave(MODES, spots)
    cos_z, sin_z = wave(np.arange(MZ), spots)
    forward_y = np.concatenate([cos_y, -sin_y], axis=0)
    forward_z = np.concatenate([cos_z, -sin_z], axis=0)
    planes = np.arange(SLABS)[:, None] * 2 + np.arange(4)[None, :]
    cos_x, sin_x = wave(MODES, planes.reshape(-1) % GRID)
    cos_x = cos_x.reshape(64, SLABS, 4)
    sin_x = sin_x.reshape(64, SLABS, 4)
    forward_x = np.zeros((2, 2, 64, SLABS, 2, 4, 2))
    inverse_x = np.zeros((SLABS, 2, 2, 2, 2, 2, 64))
    for half in range(2):
        for plane in range(3):
            c, s = cos_x[:, :, plane], sin_x[:, :, plane]
            forward_x[0, half, :, :, half, plane, 0] = c
            forward_x[0, half, :, :, half, plane, 1] = s
            forward_x[1, half, :, :, half, plane, 0] = -s
            forward_x[1, half, :, :, half, plane, 1] = c
            if plane < 2:
                inverse_x[:, half, plane, 0, half, 0] = c.T
                inverse_x[:, half, plane, 0, half, 1] = -s.T
                inverse_x[:, half, plane, 1, half, 0] = s.T
                inverse_x[:, half, plane, 1, half, 1] = c.T
    inverse_y = np.block([[cos_y.T, -sin_y.T], [sin_y.T, cos_y.T]])
    factor = np.where(np.arange(MZ) == 0, 1.0, 2.0)[:, None] / float(GRID) ** 3
    inverse_z = np.zeros((2, 4, MZ, 4, GRID))
    for group in range(4):
        inverse_z[0, group, :, group] = factor * cos_z
        inverse_z[1, group, :, group] = -factor * sin_z
    as_bf16 = lambda table, shape: np.asarray(table.reshape(shape), dtype=jnp.bfloat16)
    return (
        as_bf16(forward_y, (128, 128)),
        as_bf16(forward_z, (64, 128)),
        as_bf16(forward_x, (256, 1024)),
        as_bf16(inverse_x, (512, 256)),
        as_bf16(inverse_y, (256, 128)),
        as_bf16(inverse_z, (256, 512)),
    )


def dot(a, b):
    return jnp.dot(a, b, preferred_element_type=F32)


def dot_nt(a, b):
    return lax.dot_general(a, b, (((1,), (1,)), ((), ())), preferred_element_type=F32)


def hat(spots, position):
    return jnp.maximum(1.0 - jnp.abs(spots - position), 0.0)


def iota(shape, dim):
    return lax.broadcasted_iota(jnp.int32, shape, dim)


def exchange(src, dst, send_sem, recv_sem, me, chan):
    def send(k, carry):
        to = lax.rem(me + k, SLABS)
        pltpu.make_async_remote_copy(
            src_ref=src.at[to],
            dst_ref=dst.at[me],
            send_sem=send_sem,
            recv_sem=recv_sem,
            device_id=(to, chan),
            device_id_type=MESH,
        ).start()
        return carry

    lax.fori_loop(1, SLABS, send, 0)
    dst[pl.ds(me, 1)] = src[pl.ds(me, 1)]


def all_but_one(src, dst, send_sem, recv_sem, me, chan):
    return pltpu.make_async_remote_copy(
        src_ref=src.at[pl.ds(0, SLABS - 1)],
        dst_ref=dst.at[pl.ds(0, SLABS - 1)],
        send_sem=send_sem,
        recv_sem=recv_sem,
        device_id=(me, chan),
        device_id_type=MESH,
    )


def kernel(
    feats, coords, counts, lift, weight, skip, bias, head, head_bias,
    fwd_y, fwd_z, fwd_x, inv_x, inv_y, inv_z,
    out,
    a_send, a_recv, t_ref, own, embeds, packet, before,
    hat_y, xz, yh, lhs, rhs, stage, c_send, c_recv,
    raw, packed, d_recv, acc, e_send, e_recv, mid, skipped, spectral,
    hn, heads, back, h_send, h_recv, sums,
    w_sem, a_sem, c_sem, e_sem, h_sem, n_sem, m_send, m_recv, d_send, d_rsem, g_send, g_recv,
):
    me = lax.axis_index("slab")
    chan = lax.axis_index("chan")
    after = lax.rem(me + 1, SLABS)

    barrier = pltpu.get_barrier_semaphore()

    def greet(k, carry):
        to = lax.rem(me + k, SLABS)
        pl.semaphore_signal(barrier, inc=1, device_id=(to, chan), device_id_type=MESH)
        return carry

    lax.fori_loop(1, SLABS, greet, 0)
    for k in range(1, CHANS):
        pl.semaphore_signal(
            barrier, inc=1, device_id=(me, lax.rem(chan + k, CHANS)), device_id_type=MESH
        )
    load = pltpu.make_async_copy(weight, raw, w_sem)
    load.start()

    lane = iota((16, POINTS), 1)
    mask = jnp.where((lane & 15) == iota((16, POINTS), 0), 1.0, 0.0)
    pick = jnp.where((iota((SLABS, POINTS), 1) >> 4) == iota((SLABS, POINTS), 0), 1.0, 0.0).astype(BF16)
    embed = dot(lift[...], feats[...]).astype(BF16).astype(F32)
    spot = coords[...]
    cell = (spot >> 4).astype(F32)
    part = (spot & 15).astype(F32)
    rows = [embed[v : v + 1] for v in range(8)]
    rows += [cell[v : v + 1] for v in range(3)] + [part[v : v + 1] for v in range(3)]
    spread = [(row * mask).astype(BF16) for row in rows]
    spread += [jnp.zeros((32, POINTS), BF16)]
    sorted_ = dot_nt(pick, jnp.concatenate(spread, axis=0))
    wide = jnp.broadcast_to(counts[...].astype(F32), (SLABS, SLABS))
    here = jnp.sum(jnp.where(iota((SLABS, SLABS), 0) == iota((SLABS, SLABS), 1), wide, 0.0), axis=1, keepdims=True)
    live = (iota((SLABS, 128), 1) & 15).astype(F32) < here
    a_send[:, 0:1, :] = jnp.where(live, sorted_[:, :128], 0.0).reshape(SLABS, 1, 128)
    a_send[:, 1:2, :] = sorted_[:, 128:].reshape(SLABS, 1, 128)

    pl.semaphore_wait(barrier, SLABS - 1 + CHANS - 1)
    exchange(a_send, a_recv, a_sem.at[0], a_sem.at[1], me, chan)
    all_but_one(a_send, a_recv, a_sem.at[0], a_sem.at[1], me, chan).wait_recv()

    got = a_recv[...]
    t_ref[...] = jnp.concatenate(
        [got[:, 0:1, :].reshape(SLABS, 128), got[:, 1:2, :].reshape(SLABS, 128)], axis=0
    ).T
    low = iota((8, 128), 1) < 64
    for k in range(8):
        first = t_ref[pl.ds(k, 8, stride=16), :]
        second = t_ref[pl.ds(k + 8, 8, stride=16), :]
        values = jnp.where(low, first, pltpu.roll(second, 64, 1))
        places = jnp.where(low, pltpu.roll(first, 64, 1), second)
        lanes = pl.ds(k * 128, 128)
        own[0:8, lanes] = values
        own[8:11, lanes] = places[0:3] + (places[3:6] + 0.5) * 0.0625
    embeds[pl.ds(chan, 1)] = own[0:8, :].reshape(1, 8, POINTS)
    for k in range(1, CHANS):
        pltpu.make_async_remote_copy(
            src_ref=own.at[0:8],
            dst_ref=embeds.at[chan],
            send_sem=m_send.at[k],
            recv_sem=m_recv.at[k],
            device_id=(me, lax.rem(chan + k, CHANS)),
            device_id_type=MESH,
        ).start()

    down = iota((128, POINTS), 0).astype(F32)
    hat_own = hat(down, own[9:10, :]).astype(BF16)
    hat_y[:, 0:POINTS] = hat_own
    hat_z = hat(down, own[10:11, :]).astype(BF16)
    yh[0:128, :] = dot(fwd_y[...], hat_own)
    yh[128:192, :] = dot(fwd_z[...], hat_z)
    base = (me * 2).astype(F32)
    local = own[8:9, :] - base
    inside = jnp.where(me == SLABS - 1, 0.0, 1.0).astype(F32)
    for plane in range(3):
        along = hat(float(plane), local)
        if plane == 2:
            along = along * inside
        for part_ in range(2):
            lhs[plane * 64 : plane * 64 + 64, part_ * POINTS : (part_ + 1) * POINTS] = (
                yh[part_ * 64 : part_ * 64 + 64, :] * along
            ).astype(BF16)
    zr = yh[128:160, :]
    zi = yh[160:192, :]
    for c in range(8):
        row = own[c : c + 1, :]
        real = (zr * row).astype(BF16)
        imag = (zi * row).astype(BF16)
        rhs[c * 32 : c * 32 + 32, 0:POINTS] = real
        rhs[c * 32 : c * 32 + 32, POINTS : 2 * POINTS] = -imag
        rhs[256 + c * 32 : 256 + c * 32 + 32, 0:POINTS] = imag
        rhs[256 + c * 32 : 256 + c * 32 + 32, POINTS : 2 * POINTS] = real
    stage[...] = jnp.zeros_like(stage)
    for part_ in range(2):
        for half in range(2):
            block = part_ * 2 + half
            result = dot_nt(lhs[...], rhs[block * 128 : block * 128 + 128, :])
            for plane in range(3):
                stage[pl.ds(half * 8 + plane * 2 + part_, 64, stride=16), :] = result[
                    plane * 64 : plane * 64 + 64
                ]
    c_send[...] = stage[...].reshape(SLABS, 16, 128).astype(BF16)
    exchange(c_send, c_recv, c_sem.at[0], c_sem.at[1], me, chan)

    for k in range(1, CHANS):
        pltpu.make_async_remote_copy(
            src_ref=own.at[0:8],
            dst_ref=embeds.at[lax.rem(chan + CHANS - k, CHANS)],
            send_sem=m_send.at[k],
            recv_sem=m_recv.at[k],
            device_id=(me, chan),
            device_id_type=MESH,
        ).wait_recv()
    packet[0:8, :] = dot(skip[...], embeds[...].reshape(32, POINTS).astype(BF16))
    packet[8:16, :] = own[8:16, :]
    pass_on = pltpu.make_async_remote_copy(
        src_ref=packet,
        dst_ref=before,
        send_sem=n_sem.at[0],
        recv_sem=n_sem.at[1],
        device_id=(after, chan),
        device_id_type=MESH,
    )
    pass_on.start()
    for plane in range(2):
        xz[plane * 128 : plane * 128 + 128, 0:POINTS] = (
            hat(float(plane), local) * hat(down, own[10:11, :])
        ).astype(BF16)
    load.wait()

    def pack(step, carry):
        kind = step // 16
        rest = step % 16
        source = (rest // 4) * 8 + rest % 4
        one = raw[kind, source]
        two = raw[kind, source + 4]
        packed[kind, rest] = jnp.concatenate([one, two], axis=-1)
        return carry

    lax.fori_loop(0, 32, pack, 0)
    all_but_one(c_send, c_recv, c_sem.at[0], c_sem.at[1], me, chan).wait_recv()

    modes = dot(fwd_x[...], c_recv[...].reshape(1024, 128))
    turned = jnp.concatenate([modes[0:128].T, modes[128:256].T], axis=0).astype(BF16)
    d_recv[pl.ds(chan, 1)] = turned.reshape(1, 256, 128)

    def gather(k, owner, to):
        return pltpu.make_async_remote_copy(
            src_ref=d_recv.at[owner],
            dst_ref=d_recv.at[owner],
            send_sem=d_send.at[k],
            recv_sem=d_rsem.at[k],
            device_id=(me, to),
            device_id_type=MESH,
        )

    for k in range(1, CHANS):
        gather(k, chan, lax.rem(chan + k, CHANS)).start()

    pass_on.wait_recv()
    hat_y[:, POINTS : 2 * POINTS] = hat(down, before[9:10, :]).astype(BF16)
    prior = before[8:9, :] - base
    for plane in range(2):
        xz[plane * 128 : plane * 128 + 128, POINTS : 2 * POINTS] = (
            hat(float(plane), prior) * hat(down, before[10:11, :])
        ).astype(BF16)

    for k in range(CHANS):
        owner = lax.rem(chan + CHANS - k, CHANS)
        if k:
            gather(k, owner, chan).wait_recv()
        def mix(o, carry, k=k, owner=owner):
            if k:
                real, imag = acc[0, o], acc[1, o]
            else:
                real = imag = jnp.zeros((MZ, 128), F32)
            for group in range(4):
                at = owner * 4 + group
                wr, wi = packed[0, at, o], packed[1, at, o]
                vr = d_recv[owner, group * 32 : group * 32 + 32, :].astype(F32)
                vi = d_recv[owner, 128 + group * 32 : 128 + group * 32 + 32, :].astype(F32)
                real = real + (wr * vr - wi * vi)
                imag = imag + (wr * vi + wi * vr)
            acc[0, o] = real
            acc[1, o] = imag
            return carry

        lax.fori_loop(0, 8, mix, 0)
    low = iota((MZ, 128), 1) < 64
    mixed = []
    for o in range(8):
        real, imag = acc[0, o], acc[1, o]
        real = real + pltpu.roll(real, 64, 1)
        imag = imag + pltpu.roll(imag, 64, 1)
        mixed.append(jnp.where(low, real, imag).astype(BF16))
    mixed = jnp.concatenate(
        [jnp.concatenate(mixed[0:4], axis=0), jnp.concatenate(mixed[4:8], axis=0)], axis=1
    )
    e_send[...] = dot_nt(inv_x[...], mixed).reshape(SLABS, 8, 128)
    exchange(e_send, e_recv, e_sem.at[0], e_sem.at[1], me, chan)

    def deposit(o, carry):
        spread = jnp.concatenate(
            [
                (packet[pl.ds(o, 1), :] * hat_y[:, 0:POINTS].astype(F32)).astype(BF16),
                (before[pl.ds(o, 1), :] * hat_y[:, POINTS : 2 * POINTS].astype(F32)).astype(BF16),
            ],
            axis=1,
        )
        skipped[o] = dot_nt(spread, xz[...]) + bias[o]
        return carry

    lax.fori_loop(0, 8, deposit, 0)
    all_but_one(e_send, e_recv, e_sem.at[0], e_sem.at[1], me, chan).wait_recv()

    for row in range(8):
        block, part_ = row // 2, row % 2
        mid[part_ * 64 : part_ * 64 + 64, block * 128 : block * 128 + 128] = (
            e_recv[:, row : row + 1, :].reshape(SLABS, 128).astype(BF16)
        )
    lines = dot(inv_y[...], mid[...]).astype(BF16)
    for half in range(2):
        for plane in range(2):
            block = half * 2 + plane
            both = jnp.concatenate(
                [
                    lines[0:128, block * 128 : block * 128 + 128],
                    lines[128:256, block * 128 : block * 128 + 128],
                ],
                axis=1,
            )
            result = dot(both, inv_z[...])
            for group in range(4):
                spectral[half * 4 + group, :, plane * 128 : plane * 128 + 128] = result[
                    :, group * 128 : group * 128 + 128
                ]

    heading = head[...].astype(F32)
    shape = (32, 256)
    scale = math.sqrt(2.0 / math.pi)

    def activate(step, carry):
        at = pl.ds(step * 32, 32)
        fields = [jnp.zeros(shape, F32) for _ in range(4)]
        for o in range(8):
            x = spectral[o, at, :] + skipped[o, at, :]
            h = 0.5 * x * (1.0 + jnp.tanh(scale * (x + 0.044715 * (x * x * x))))
            for n in range(4):
                fields[n] = fields[n] + jnp.broadcast_to(heading[n : n + 1, o : o + 1], shape) * h
        for n in range(4):
            hn[n, at, :] = fields[n].astype(BF16)
        return carry

    lax.fori_loop(0, 4, activate, 0)

    fields = hn[...].reshape(512, 256)
    for block in range(8):
        lanes = pl.ds(block * 256, 256)
        along_z = dot(fields, xz[:, lanes])
        weights = hat_y[:, lanes].astype(F32)
        for n in range(4):
            sampled = jnp.sum(along_z[n * 128 : n * 128 + 128] * weights, axis=0, keepdims=True)
            which = block // 4
            heads[which * 4 + n : which * 4 + n + 1, pl.ds((block % 4) * 256, 256)] = sampled
    for k in range(8):
        piece = heads[:, k * 128 : k * 128 + 128]
        back[pl.ds(k, 8, stride=16), :] = piece
        back[pl.ds(k + 8, 8, stride=16), :] = pltpu.roll(piece, 64, 1)
    h_send[...] = back[...].T[0:SLABS].reshape(SLABS, 1, 128)
    exchange(h_send, h_recv, h_sem.at[0], h_sem.at[1], me, chan)
    all_but_one(h_send, h_recv, h_sem.at[0], h_sem.at[1], me, chan).wait_recv()

    home = h_recv[...].reshape(SLABS, 128)
    home = home + pltpu.roll(pltpu.roll(home, SLABS - 1, 0), 64, 1)
    sums[pl.ds(chan, 1)] = home.reshape(1, SLABS, 128)

    def total(k, owner, to):
        return pltpu.make_async_remote_copy(
            src_ref=sums.at[owner],
            dst_ref=sums.at[owner],
            send_sem=g_send.at[k],
            recv_sem=g_recv.at[k],
            device_id=(me, to),
            device_id_type=MESH,
        )

    for k in range(1, CHANS):
        total(k, chan, lax.rem(chan + k, CHANS)).start()
    pick2 = jnp.where((iota((SLABS, POINTS), 1) >> 4) == iota((SLABS, POINTS), 0), 1.0, 0.0).astype(BF16)
    cover = dot(jnp.broadcast_to(counts[...].astype(F32), (8, SLABS)).astype(BF16), pick2)
    alive = (iota((4, POINTS), 1) & 15).astype(F32) < cover[0:4]
    for k in range(1, CHANS):
        total(k, lax.rem(chan + CHANS - k, CHANS), chan).wait_recv()
    home = sums[0] + sums[1] + sums[2] + sums[3]
    turned = jnp.concatenate([home, jnp.zeros_like(home)], axis=0).T[0:SLABS, 0:SLABS]
    top = turned.astype(BF16)
    rest = turned - top.astype(F32)
    middle = rest.astype(BF16)
    bottom = (rest - middle.astype(F32)).astype(BF16)
    laid = dot(top, pick2) + dot(middle, pick2) + dot(bottom, pick2)
    for n in range(4):
        line = jnp.sum(laid[n * 16 : n * 16 + 16] * mask, axis=0, keepdims=True)
        out[n : n + 1, :] = jnp.where(alive[n : n + 1], line + head_bias[n], 0.0)

    for pair, src, dst in ((a_sem, a_send, a_recv), (c_sem, c_send, c_recv), (e_sem, e_send, e_recv), (h_sem, h_send, h_recv)):
        all_but_one(src, dst, pair.at[0], pair.at[1], me, chan).wait_send()
    pass_on.wait_send()
    for k in range(1, CHANS):
        pltpu.make_async_remote_copy(
            src_ref=own.at[0:8],
            dst_ref=embeds.at[chan],
            send_sem=m_send.at[k],
            recv_sem=m_recv.at[k],
            device_id=(me, chan),
            device_id_type=MESH,
        ).wait_send()
        gather(k, chan, chan).wait_send()
        total(k, chan, chan).wait_send()


def local(
    point_feats, cell_coords, send_counts, lift_weight, spec_weight,
    skip_weight, spec_bias, out_weight, out_bias,
):
    weight = jnp.swapaxes(spec_weight, 4, 5).reshape(2, 32, 8, MZ, 64)
    vmem = pl.BlockSpec(memory_space=pltpu.VMEM)
    smem = pl.BlockSpec(memory_space=pltpu.SMEM)
    hbm = pl.BlockSpec(memory_space=pl.ANY)
    dma = pltpu.SemaphoreType.DMA
    scratch = [
        pltpu.VMEM((SLABS, 2, 128), F32),
        pltpu.VMEM((SLABS, 2, 128), F32),
        pltpu.VMEM((128, 128), F32),
        pltpu.VMEM((16, POINTS), F32),
        pltpu.VMEM((CHANS, 8, POINTS), F32),
        pltpu.VMEM((16, POINTS), F32),
        pltpu.VMEM((16, POINTS), F32),
        pltpu.VMEM((128, 2 * POINTS), BF16),
        pltpu.VMEM((256, 2 * POINTS), BF16),
        pltpu.VMEM((192, POINTS), F32),
        pltpu.VMEM((192, 2 * POINTS), BF16),
        pltpu.VMEM((512, 2 * POINTS), BF16),
        pltpu.VMEM((1024, 128), F32),
        pltpu.VMEM((SLABS, 16, 128), BF16),
        pltpu.VMEM((SLABS, 16, 128), BF16),
        pltpu.VMEM((2, 32, 8, MZ, 64), F32),
        pltpu.VMEM((2, 16, 8, MZ, 128), F32),
        pltpu.VMEM((CHANS, 256, 128), BF16),
        pltpu.VMEM((2, 8, MZ, 128), F32),
        pltpu.VMEM((SLABS, 8, 128), F32),
        pltpu.VMEM((SLABS, 8, 128), F32),
        pltpu.VMEM((128, 512), BF16),
        pltpu.VMEM((8, 128, 256), F32),
        pltpu.VMEM((8, 128, 256), F32),
        pltpu.VMEM((4, 128, 256), BF16),
        pltpu.VMEM((8, POINTS), F32),
        pltpu.VMEM((128, 128), F32),
        pltpu.VMEM((SLABS, 1, 128), F32),
        pltpu.VMEM((SLABS, 1, 128), F32),
        pltpu.VMEM((CHANS, SLABS, 128), F32),
        dma,
        dma((2,)),
        dma((2,)),
        dma((2,)),
        dma((2,)),
        dma((2,)),
        dma((CHANS,)),
        dma((CHANS,)),
        dma((CHANS,)),
        dma((CHANS,)),
        dma((CHANS,)),
        dma((CHANS,)),
    ]
    return pl.pallas_call(
        kernel,
        out_shape=jax.ShapeDtypeStruct((4, POINTS), F32),
        in_specs=[vmem, vmem, vmem, vmem, hbm, vmem, smem, vmem, smem] + [vmem] * 6,
        out_specs=vmem,
        scratch_shapes=scratch,
        compiler_params=pltpu.CompilerParams(
            collective_id=0, has_side_effects=True, vmem_limit_bytes=48 * 1024 * 1024
        ),
    )(
        point_feats, cell_coords, send_counts, lift_weight.T, weight,
        skip_weight.T, spec_bias, out_weight.T, out_bias, *(jnp.asarray(t) for t in tables()),
    )


def solution(mesh):
    in_specs = (
        P(None, "slab"),
        P(None, "slab"),
        P("slab", None),
        P(None, "chan"),
        P(None, None, "chan", "slab", None, None),
        P(None, "chan"),
        P("chan"),
        P("chan", None),
        P(),
    )
    out_specs = P(None, "slab")
    return jax.shard_map(local, mesh=mesh, in_specs=in_specs, out_specs=out_specs, check_vma=False)
```

```python
import functools
import math

import jax
import jax.numpy as jnp
import numpy as np
from jax import lax
from jax.experimental import pallas as pl
from jax.experimental.pallas import tpu as pltpu
from jax.sharding import PartitionSpec as P

GRID = 128
MZ = 32
CAP = 16
SLABS = 64
CHANS = 4
POINTS = 1024
MODES = np.concatenate([np.arange(MZ), np.arange(GRID - MZ, GRID)])
MESH = pl.DeviceIdType.MESH
F32 = jnp.float32
BF16 = jnp.bfloat16


def wave(freqs, positions):
    angle = (freqs[:, None] * positions[None, :] % GRID) * (2.0 * math.pi / GRID)
    return np.cos(angle), np.sin(angle)


def tables():
    spots = np.arange(GRID)
    cos_y, sin_y = wave(MODES, spots)
    cos_z, sin_z = wave(np.arange(MZ), spots)
    forward_y = np.concatenate([cos_y, -sin_y], axis=0)
    forward_z = np.concatenate([cos_z, -sin_z], axis=0)
    planes = np.arange(SLABS)[:, None] * 2 + np.arange(2)[None, :]
    cos_x, sin_x = wave(MODES, planes.reshape(-1) % GRID)
    cos_x = cos_x.reshape(64, SLABS, 2)
    sin_x = sin_x.reshape(64, SLABS, 2)
    forward_x = np.zeros((2, 2, 64, SLABS, 2, 2, 2))
    inverse_x = np.zeros((SLABS, 2, 2, 2, 2, 2, 64))
    for half in range(2):
        for plane in range(2):
            c, s = cos_x[:, :, plane], sin_x[:, :, plane]
            forward_x[0, half, :, :, half, plane, 0] = c
            forward_x[0, half, :, :, half, plane, 1] = s
            forward_x[1, half, :, :, half, plane, 0] = -s
            forward_x[1, half, :, :, half, plane, 1] = c
            inverse_x[:, half, plane, 0, half, 0] = c.T
            inverse_x[:, half, plane, 0, half, 1] = -s.T
            inverse_x[:, half, plane, 1, half, 0] = s.T
            inverse_x[:, half, plane, 1, half, 1] = c.T
    inverse_y = np.zeros((4, 2, GRID, 64, 4, 2))
    for block in range(4):
        inverse_y[block, 0, :, :, block, 0] = cos_y.T
        inverse_y[block, 0, :, :, block, 1] = -sin_y.T
        inverse_y[block, 1, :, :, block, 0] = sin_y.T
        inverse_y[block, 1, :, :, block, 1] = cos_y.T
    factor = np.where(np.arange(MZ) == 0, 1.0, 2.0)[:, None] / float(GRID) ** 3
    inverse_z = np.zeros((2, 4, MZ, 4, GRID))
    for group in range(4):
        inverse_z[0, group, :, group] = factor * cos_z
        inverse_z[1, group, :, group] = -factor * sin_z
    as_bf16 = lambda table, shape: np.asarray(table.reshape(shape), dtype=jnp.bfloat16)
    return (
        as_bf16(np.concatenate([forward_y, forward_z], axis=0), (192, 128)),
        as_bf16(forward_x, (256, 512)),
        as_bf16(inverse_x, (512, 256)),
        as_bf16(inverse_y, (1024, 512)),
        as_bf16(inverse_z, (256, 512)),
    )


def dot(a, b):
    return jnp.dot(a, b, preferred_element_type=F32)


def dot_nt(a, b):
    return lax.dot_general(a, b, (((1,), (1,)), ((), ())), preferred_element_type=F32)


def hat(spots, position):
    return jnp.maximum(1.0 - jnp.abs(spots - position), 0.0)


def iota(shape, dim):
    return lax.broadcasted_iota(jnp.int32, shape, dim)


def exchange(src, dst, send_sem, recv_sem, me, chan):
    def send(k, carry):
        to = lax.rem(me + k, SLABS)
        pltpu.make_async_remote_copy(
            src_ref=src.at[to],
            dst_ref=dst.at[me],
            send_sem=send_sem,
            recv_sem=recv_sem,
            device_id=(to, chan),
            device_id_type=MESH,
        ).start()
        return carry

    lax.fori_loop(1, SLABS, send, 0)
    dst[pl.ds(me, 1)] = src[pl.ds(me, 1)]


def all_but_one(src, dst, send_sem, recv_sem, me, chan):
    return pltpu.make_async_remote_copy(
        src_ref=src.at[pl.ds(0, SLABS - 1)],
        dst_ref=dst.at[pl.ds(0, SLABS - 1)],
        send_sem=send_sem,
        recv_sem=recv_sem,
        device_id=(me, chan),
        device_id_type=MESH,
    )


def kernel(
    feats_in, coords_in, counts_in, lift_in, weight, skip_in, bias_in, head_in, head_bias_in,
    fwd_yz_in, fwd_x_in, inv_x_in, inv_y_in, inv_z_in,
    out,
    feats, coords, counts, lift, skip, bias, head, head_bias,
    fwd_yz, fwd_x, inv_x, inv_y, inv_z,
    a_send, a_recv, t_ref, own, prior, embeds, packet, before, along,
    hat_y, hat_z, yh, lhs, rhs, stage, c_send, c_recv,
    raw, packed, d_recv, acc, e_send, e_recv, skipped, spectral,
    hn, heads, back, h_send, h_recv, sums,
    load_sem, a_sem, c_sem, e_sem, h_sem, n_sem, s_sem, m_send, m_recv, d_send, d_rsem, g_send, g_recv,
):
    me = lax.axis_index("slab")
    chan = lax.axis_index("chan")
    after = lax.rem(me + 1, SLABS)

    loads = {}
    for k, (name, src, dst) in enumerate((
        ("feats", feats_in, feats), ("coords", coords_in, coords), ("counts", counts_in, counts),
        ("lift", lift_in, lift), ("fwd_yz", fwd_yz_in, fwd_yz), ("skip", skip_in, skip),
        ("weight", weight, raw), ("fwd_x", fwd_x_in, fwd_x), ("inv_x", inv_x_in, inv_x),
        ("inv_y", inv_y_in, inv_y), ("inv_z", inv_z_in, inv_z), ("bias", bias_in, bias),
        ("head", head_in, head), ("head_bias", head_bias_in, head_bias),
    )):
        loads[name] = pltpu.make_async_copy(src, dst, load_sem.at[k])

    barrier = pltpu.get_barrier_semaphore()

    def greet(k, carry):
        to = lax.rem(me + k, SLABS)
        pl.semaphore_signal(barrier, inc=1, device_id=(to, chan), device_id_type=MESH)
        return carry

    lax.fori_loop(1, SLABS, greet, 0)
    for k in range(1, CHANS):
        pl.semaphore_signal(
            barrier, inc=1, device_id=(me, lax.rem(chan + k, CHANS)), device_id_type=MESH
        )
    for load in loads.values():
        load.start()
    pending = []
    for name in ("feats", "coords", "counts", "lift"):
        loads[name].wait()

    lane = iota((16, POINTS), 1)
    mask = jnp.where((lane & 15) == iota((16, POINTS), 0), 1.0, 0.0)
    pick = jnp.where((iota((SLABS, POINTS), 1) >> 4) == iota((SLABS, POINTS), 0), 1.0, 0.0).astype(BF16)
    embed = dot(lift[...], feats[...]).astype(BF16).astype(F32)
    spot = coords[...]
    cell = (spot >> 4).astype(F32)
    part = (spot & 15).astype(F32)
    rows = [embed[v : v + 1] for v in range(8)]
    rows += [cell[v : v + 1] for v in range(3)] + [part[v : v + 1] for v in range(3)]
    spread = [(row * mask).astype(BF16) for row in rows]
    spread += [jnp.zeros((32, POINTS), BF16)]
    sorted_ = dot_nt(pick, jnp.concatenate(spread, axis=0))
    wide = jnp.broadcast_to(counts[...].astype(F32), (SLABS, SLABS))
    here = jnp.sum(jnp.where(iota((SLABS, SLABS), 0) == iota((SLABS, SLABS), 1), wide, 0.0), axis=1, keepdims=True)
    live = (iota((SLABS, 128), 1) & 15).astype(F32) < here
    a_send[:, 0:1, :] = jnp.where(live, sorted_[:, :128], 0.0).reshape(SLABS, 1, 128)
    a_send[:, 1:2, :] = sorted_[:, 128:].reshape(SLABS, 1, 128)

    pl.semaphore_wait(barrier, SLABS - 1 + CHANS - 1)
    exchange(a_send, a_recv, a_sem.at[0], a_sem.at[1], me, chan)
    a_all = all_but_one(a_send, a_recv, a_sem.at[0], a_sem.at[1], me, chan)
    pending.append(a_all)
    a_all.wait_recv()

    got = a_recv[...]
    t_ref[...] = jnp.concatenate(
        [got[:, 0:1, :].reshape(SLABS, 128), got[:, 1:2, :].reshape(SLABS, 128)], axis=0
    ).T
    low = iota((8, 128), 1) < 64
    for k in range(8):
        first = t_ref[pl.ds(k, 8, stride=16), :]
        second = t_ref[pl.ds(k + 8, 8, stride=16), :]
        values = jnp.where(low, first, pltpu.roll(second, 64, 1))
        places = jnp.where(low, pltpu.roll(first, 64, 1), second)
        lanes = pl.ds(k * 128, 128)
        own[0:8, lanes] = values
        own[8:11, lanes] = places[0:3] + (places[3:6] + 0.5) * 0.0625
        own[11:16, lanes] = places[3:8]
    pass_on = pltpu.make_async_remote_copy(
        src_ref=own,
        dst_ref=prior,
        send_sem=n_sem.at[0],
        recv_sem=n_sem.at[1],
        device_id=(after, chan),
        device_id_type=MESH,
    )
    pass_on.start()
    pending.append(pass_on)
    embeds[pl.ds(chan, 1)] = own[0:8, :].reshape(1, 8, POINTS)

    def share(k, owner, to):
        return pltpu.make_async_remote_copy(
            src_ref=own.at[0:8],
            dst_ref=embeds.at[owner],
            send_sem=m_send.at[k],
            recv_sem=m_recv.at[k],
            device_id=(me, to),
            device_id_type=MESH,
        )

    for k in range(1, CHANS):
        share(k, chan, lax.rem(chan + k, CHANS)).start()
        pending.append(share(k, chan, chan))

    loads["fwd_yz"].wait()
    base = (me * 2).astype(F32)
    down = iota((128, POINTS), 0).astype(F32)

    def transform(points, which):
        lanes = slice(which * POINTS, (which + 1) * POINTS)
        hat_y[:, lanes] = hat(down, points[9:10, :]).astype(BF16)
        hat_z[:, lanes] = hat(down, points[10:11, :]).astype(BF16)
        yh[0:128, :] = dot(fwd_yz[0:128, :], hat_y[:, lanes])
        yh[128:192, :] = dot(fwd_yz[128:192, :], hat_z[:, lanes])
        local = points[8:9, :] - base
        planes = 2 - which
        for plane in range(planes):
            near = hat(float(plane), local)
            along[plane : plane + 1, lanes] = near
            for part_ in range(2):
                lhs[plane * 64 : plane * 64 + 64, part_ * POINTS : (part_ + 1) * POINTS] = (
                    yh[part_ * 64 : part_ * 64 + 64, :] * near
                ).astype(BF16)
        zr = yh[128:160, :]
        zi = yh[160:192, :]
        for c in range(8):
            row = points[c : c + 1, :]
            real = (zr * row).astype(BF16)
            imag = (zi * row).astype(BF16)
            rhs[c * 32 : c * 32 + 32, 0:POINTS] = real
            rhs[c * 32 : c * 32 + 32, POINTS : 2 * POINTS] = -imag
            rhs[256 + c * 32 : 256 + c * 32 + 32, 0:POINTS] = imag
            rhs[256 + c * 32 : 256 + c * 32 + 32, POINTS : 2 * POINTS] = real
        for part_ in range(2):
            for half in range(2):
                block = part_ * 2 + half
                result = dot_nt(lhs[0 : planes * 64], rhs[block * 128 : block * 128 + 128, :])
                for plane in range(planes):
                    rows = pl.ds(half * 4 + plane * 2 + part_, 64, stride=8)
                    piece = result[plane * 64 : plane * 64 + 64]
                    stage[rows, :] = stage[rows, :] + piece if which else piece

    transform(own, 0)
    pass_on.wait_recv()
    transform(prior, 1)
    c_send[...] = stage[...].reshape(SLABS, 8, 128).astype(BF16)
    exchange(c_send, c_recv, c_sem.at[0], c_sem.at[1], me, chan)
    c_all = all_but_one(c_send, c_recv, c_sem.at[0], c_sem.at[1], me, chan)
    pending.append(c_all)

    for k in range(1, CHANS):
        share(k, lax.rem(chan + CHANS - k, CHANS), chan).wait_recv()
    loads["skip"].wait()
    packet[...] = dot(skip[...], embeds[...].reshape(32, POINTS).astype(BF16))
    skip_on = pltpu.make_async_remote_copy(
        src_ref=packet,
        dst_ref=before,
        send_sem=s_sem.at[0],
        recv_sem=s_sem.at[1],
        device_id=(after, chan),
        device_id_type=MESH,
    )
    skip_on.start()
    pending.append(skip_on)
    loads["weight"].wait()

    def pack(step, carry):
        kind = step // 16
        rest = step % 16
        source = (rest // 4) * 8 + rest % 4
        one = raw[kind, source]
        two = raw[kind, source + 4]
        packed[kind, rest] = jnp.concatenate([one, two], axis=-1)
        return carry

    lax.fori_loop(0, 32, pack, 0)
    c_all.wait_recv()

    loads["fwd_x"].wait()
    modes = dot(fwd_x[...], c_recv[...].astype(F32).reshape(512, 128).astype(BF16))
    turned = jnp.concatenate([modes[0:128].T, modes[128:256].T], axis=0).astype(BF16)
    d_recv[pl.ds(chan, 1)] = turned.reshape(1, 256, 128)

    def gather(k, owner, to):
        return pltpu.make_async_remote_copy(
            src_ref=d_recv.at[owner],
            dst_ref=d_recv.at[owner],
            send_sem=d_send.at[k],
            recv_sem=d_rsem.at[k],
            device_id=(me, to),
            device_id_type=MESH,
        )

    for k in range(1, CHANS):
        gather(k, chan, lax.rem(chan + k, CHANS)).start()
        pending.append(gather(k, chan, chan))

    for k in (0, 1, 3, 2):
        owner = lax.rem(chan + CHANS - k, CHANS)
        if k:
            gather(k, owner, chan).wait_recv()
        def mix(o, carry, k=k, owner=owner):
            if k:
                real, imag = acc[0, o], acc[1, o]
            else:
                real = imag = jnp.zeros((MZ, 128), F32)
            for group in range(4):
                at = owner * 4 + group
                wr, wi = packed[0, at, o], packed[1, at, o]
                vr = d_recv[owner, group * 32 : group * 32 + 32, :].astype(F32)
                vi = d_recv[owner, 128 + group * 32 : 128 + group * 32 + 32, :].astype(F32)
                real = real + (wr * vr - wi * vi)
                imag = imag + (wr * vi + wi * vr)
            acc[0, o] = real
            acc[1, o] = imag
            return carry

        lax.fori_loop(0, 8, mix, 0)
    low = iota((MZ, 128), 1) < 64
    mixed = []
    for o in range(8):
        real, imag = acc[0, o], acc[1, o]
        real = real + pltpu.roll(real, 64, 1)
        imag = imag + pltpu.roll(imag, 64, 1)
        mixed.append(jnp.where(low, real, imag).astype(BF16))
    mixed = jnp.concatenate(
        [jnp.concatenate(mixed[0:4], axis=0), jnp.concatenate(mixed[4:8], axis=0)], axis=1
    )
    loads["inv_x"].wait()
    e_send[...] = dot_nt(inv_x[...], mixed).reshape(SLABS, 8, 128).astype(BF16)
    exchange(e_send, e_recv, e_sem.at[0], e_sem.at[1], me, chan)
    e_all = all_but_one(e_send, e_recv, e_sem.at[0], e_sem.at[1], me, chan)
    pending.append(e_all)

    skip_on.wait_recv()
    loads["bias"].wait()

    def deposit(o, carry):
        first = jnp.concatenate([packet[pl.ds(o, 1), :], before[pl.ds(o, 1), :]], axis=1)
        for plane in range(2):
            width = (2 - plane) * POINTS
            spread = hat_y[:, 0:width].astype(F32) * (first[:, 0:width] * along[plane : plane + 1, 0:width])
            high = spread.astype(BF16)
            rest = (spread - high.astype(F32)).astype(BF16)
            grid_z = hat_z[:, 0:width]
            skipped[o, :, plane * 128 : plane * 128 + 128] = (
                dot_nt(high, grid_z) + dot_nt(rest, grid_z) + bias[o]
            )
        return carry

    lax.fori_loop(0, 8, deposit, 0)
    e_all.wait_recv()

    loads["inv_y"].wait()
    loads["inv_z"].wait()
    lines = dot(inv_y[...], e_recv[...].astype(F32).reshape(512, 128).astype(BF16)).astype(BF16)
    for block in range(4):
        half, plane = block // 2, block % 2
        at = block * 256
        both = jnp.concatenate([lines[at : at + 128], lines[at + 128 : at + 256]], axis=1)
        result = dot(both, inv_z[...])
        for group in range(4):
            spectral[half * 4 + group, :, plane * 128 : plane * 128 + 128] = result[
                :, group * 128 : group * 128 + 128
            ]

    loads["head"].wait()
    loads["head_bias"].wait()
    heading = head[...].astype(F32)
    shape = (32, 256)
    scale = math.sqrt(2.0 / math.pi)

    def activate(step, carry):
        at = pl.ds(step * 32, 32)
        fields = [jnp.zeros(shape, F32) for _ in range(4)]
        for o in range(8):
            x = spectral[o, at, :] + skipped[o, at, :]
            h = 0.5 * x * (1.0 + jnp.tanh(scale * (x + 0.044715 * (x * x * x))))
            for n in range(4):
                fields[n] = fields[n] + jnp.broadcast_to(heading[n : n + 1, o : o + 1], shape) * h
        for n in range(4):
            high = fields[n].astype(BF16)
            rest = (fields[n] - high.astype(F32)).astype(BF16)
            for plane in range(2):
                z = slice(plane * 128, plane * 128 + 128)
                hn[plane, n, at, 0:128] = high[:, z]
                hn[plane, n, at, 128:256] = rest[:, z]
        return carry

    lax.fori_loop(0, 4, activate, 0)

    fields = hn[...].reshape(1024, 256)
    for block in range(8):
        lanes = pl.ds(block * 256, 256)
        planes = 2 if block < 4 else 1
        grid_z = hat_z[:, lanes]
        along_z = dot(fields[0 : planes * 512], jnp.concatenate([grid_z, grid_z], axis=0))
        grid_y = hat_y[:, lanes].astype(F32)
        for n in range(4):
            sampled = jnp.zeros((1, 256), F32)
            for plane in range(planes):
                at = plane * 512 + n * 128
                line = jnp.sum(along_z[at : at + 128] * grid_y, axis=0, keepdims=True)
                sampled = sampled + line * along[plane : plane + 1, lanes]
            which = block // 4
            heads[which * 4 + n : which * 4 + n + 1, pl.ds((block % 4) * 256, 256)] = sampled
    for k in range(8):
        piece = heads[:, k * 128 : k * 128 + 128]
        back[pl.ds(k, 8, stride=16), :] = piece
        back[pl.ds(k + 8, 8, stride=16), :] = pltpu.roll(piece, 64, 1)
    h_send[...] = back[...].T[0:SLABS].reshape(SLABS, 1, 128)
    exchange(h_send, h_recv, h_sem.at[0], h_sem.at[1], me, chan)
    h_all = all_but_one(h_send, h_recv, h_sem.at[0], h_sem.at[1], me, chan)
    pending.append(h_all)
    h_all.wait_recv()

    home = h_recv[...].reshape(SLABS, 128)
    home = home + pltpu.roll(pltpu.roll(home, SLABS - 1, 0), 64, 1)
    sums[pl.ds(chan, 1)] = home.reshape(1, SLABS, 128)

    def total(k, owner, to):
        return pltpu.make_async_remote_copy(
            src_ref=sums.at[owner],
            dst_ref=sums.at[owner],
            send_sem=g_send.at[k],
            recv_sem=g_recv.at[k],
            device_id=(me, to),
            device_id_type=MESH,
        )

    for k in range(1, CHANS):
        total(k, chan, lax.rem(chan + k, CHANS)).start()
        pending.append(total(k, chan, chan))
    pick2 = jnp.where((iota((SLABS, POINTS), 1) >> 4) == iota((SLABS, POINTS), 0), 1.0, 0.0).astype(BF16)
    cover = dot(jnp.broadcast_to(counts[...].astype(F32), (8, SLABS)).astype(BF16), pick2)
    alive = (iota((4, POINTS), 1) & 15).astype(F32) < cover[0:4]
    for k in range(1, CHANS):
        total(k, lax.rem(chan + CHANS - k, CHANS), chan).wait_recv()
    home = sums[0] + sums[1] + sums[2] + sums[3]
    turned = jnp.concatenate([home, jnp.zeros_like(home)], axis=0).T[0:SLABS, 0:SLABS]
    top = turned.astype(BF16)
    rest = turned - top.astype(F32)
    middle = rest.astype(BF16)
    bottom = (rest - middle.astype(F32)).astype(BF16)
    laid = dot(top, pick2) + dot(middle, pick2) + dot(bottom, pick2)
    for n in range(4):
        line = jnp.sum(laid[n * 16 : n * 16 + 16] * mask, axis=0, keepdims=True)
        out[n : n + 1, :] = jnp.where(alive[n : n + 1], line + head_bias[n], 0.0)

    for copy in pending:
        copy.wait_send()


def local(
    point_feats, cell_coords, send_counts, lift_weight, spec_weight,
    skip_weight, spec_bias, out_weight, out_bias,
):
    weight = jnp.swapaxes(spec_weight, 4, 5).reshape(2, 32, 8, MZ, 64)
    vmem = pl.BlockSpec(memory_space=pltpu.VMEM)
    hbm = pl.BlockSpec(memory_space=pltpu.HBM)
    dma = pltpu.SemaphoreType.DMA
    scratch = [
        pltpu.VMEM((32, POINTS), BF16),
        pltpu.VMEM((3, POINTS), jnp.int32),
        pltpu.VMEM((1, SLABS), jnp.int32),
        pltpu.VMEM((8, 32), BF16),
        pltpu.VMEM((8, 32), BF16),
        pltpu.SMEM((8,), F32),
        pltpu.VMEM((4, 8), BF16),
        pltpu.SMEM((4,), F32),
        pltpu.VMEM((192, 128), BF16),
        pltpu.VMEM((256, 512), BF16),
        pltpu.VMEM((512, 256), BF16),
        pltpu.VMEM((1024, 512), BF16),
        pltpu.VMEM((256, 512), BF16),
        pltpu.VMEM((SLABS, 2, 128), F32),
        pltpu.VMEM((SLABS, 2, 128), F32),
        pltpu.VMEM((128, 128), F32),
        pltpu.VMEM((16, POINTS), F32),
        pltpu.VMEM((16, POINTS), F32),
        pltpu.VMEM((CHANS, 8, POINTS), F32),
        pltpu.VMEM((8, POINTS), F32),
        pltpu.VMEM((8, POINTS), F32),
        pltpu.VMEM((8, 2 * POINTS), F32),
        pltpu.VMEM((128, 2 * POINTS), BF16),
        pltpu.VMEM((128, 2 * POINTS), BF16),
        pltpu.VMEM((192, POINTS), F32),
        pltpu.VMEM((128, 2 * POINTS), BF16),
        pltpu.VMEM((512, 2 * POINTS), BF16),
        pltpu.VMEM((512, 128), F32),
        pltpu.VMEM((SLABS, 8, 128), BF16),
        pltpu.VMEM((SLABS, 8, 128), BF16),
        pltpu.VMEM((2, 32, 8, MZ, 64), F32),
        pltpu.VMEM((2, 16, 8, MZ, 128), F32),
        pltpu.VMEM((CHANS, 256, 128), BF16),
        pltpu.VMEM((2, 8, MZ, 128), F32),
        pltpu.VMEM((SLABS, 8, 128), BF16),
        pltpu.VMEM((SLABS, 8, 128), BF16),
        pltpu.VMEM((8, 128, 256), F32),
        pltpu.VMEM((8, 128, 256), F32),
        pltpu.VMEM((2, 4, 128, 256), BF16),
        pltpu.VMEM((8, POINTS), F32),
        pltpu.VMEM((128, 128), F32),
        pltpu.VMEM((SLABS, 1, 128), F32),
        pltpu.VMEM((SLABS, 1, 128), F32),
        pltpu.VMEM((CHANS, SLABS, 128), F32),
        dma((14,)),
        dma((2,)),
        dma((2,)),
        dma((2,)),
        dma((2,)),
        dma((2,)),
        dma((2,)),
        dma((CHANS,)),
        dma((CHANS,)),
        dma((CHANS,)),
        dma((CHANS,)),
        dma((CHANS,)),
        dma((CHANS,)),
    ]
    return pl.pallas_call(
        kernel,
        out_shape=jax.ShapeDtypeStruct((4, POINTS), F32),
        in_specs=[hbm] * 14,
        out_specs=vmem,
        scratch_shapes=scratch,
        compiler_params=pltpu.CompilerParams(
            collective_id=0, has_side_effects=True, vmem_limit_bytes=60 * 1024 * 1024
        ),
    )(
        point_feats, cell_coords, send_counts, lift_weight.T, weight,
        skip_weight.T, spec_bias, out_weight.T, out_bias, *(jnp.asarray(t) for t in tables()),
    )


def solution(mesh):
    in_specs = (
        P(None, "slab"),
        P(None, "slab"),
        P("slab", None),
        P(None, "chan"),
        P(None, None, "chan", "slab", None, None),
        P(None, "chan"),
        P("chan"),
        P("chan", None),
        P(),
    )
    out_specs = P(None, "slab")
    return jax.shard_map(local, mesh=mesh, in_specs=in_specs, out_specs=out_specs, check_vma=False)
```

```python
import functools
import math

import jax
import jax.numpy as jnp
import numpy as np
from jax import lax
from jax.experimental import pallas as pl
from jax.experimental.pallas import tpu as pltpu
from jax.sharding import PartitionSpec as P

GRID = 128
MZ = 32
CAP = 16
SLABS = 64
CHANS = 4
POINTS = 1024
DEPOSIT_C = 3
DEPOSIT_D = 6
MODES = np.concatenate([np.arange(MZ), np.arange(GRID - MZ, GRID)])
MESH = pl.DeviceIdType.MESH
F32 = jnp.float32
BF16 = jnp.bfloat16


def wave(freqs, positions):
    angle = (freqs[:, None] * positions[None, :] % GRID) * (2.0 * math.pi / GRID)
    return np.cos(angle), np.sin(angle)


def tables():
    spots = np.arange(GRID)
    cos_y, sin_y = wave(MODES, spots)
    cos_z, sin_z = wave(np.arange(MZ), spots)
    forward_y = np.concatenate([cos_y, -sin_y], axis=0)
    forward_z = np.concatenate([cos_z, -sin_z], axis=0)
    planes = np.arange(SLABS)[:, None] * 2 + np.arange(2)[None, :]
    cos_x, sin_x = wave(MODES, planes.reshape(-1) % GRID)
    cos_x = cos_x.reshape(64, SLABS, 2)
    sin_x = sin_x.reshape(64, SLABS, 2)
    forward_x = np.zeros((2, 2, 64, SLABS, 2, 2, 2))
    inverse_x = np.zeros((SLABS, 2, 2, 2, 2, 2, 64))
    for half in range(2):
        for plane in range(2):
            c, s = cos_x[:, :, plane], sin_x[:, :, plane]
            forward_x[0, half, :, :, half, plane, 0] = c
            forward_x[0, half, :, :, half, plane, 1] = s
            forward_x[1, half, :, :, half, plane, 0] = -s
            forward_x[1, half, :, :, half, plane, 1] = c
            inverse_x[:, half, plane, 0, half, 0] = c.T
            inverse_x[:, half, plane, 0, half, 1] = -s.T
            inverse_x[:, half, plane, 1, half, 0] = s.T
            inverse_x[:, half, plane, 1, half, 1] = c.T
    inverse_y = np.zeros((4, 2, GRID, 64, 4, 2))
    for block in range(4):
        inverse_y[block, 0, :, :, block, 0] = cos_y.T
        inverse_y[block, 0, :, :, block, 1] = -sin_y.T
        inverse_y[block, 1, :, :, block, 0] = sin_y.T
        inverse_y[block, 1, :, :, block, 1] = cos_y.T
    factor = np.where(np.arange(MZ) == 0, 1.0, 2.0)[:, None] / float(GRID) ** 3
    inverse_z = np.zeros((2, 4, MZ, 4, GRID))
    for group in range(4):
        inverse_z[0, group, :, group] = factor * cos_z
        inverse_z[1, group, :, group] = -factor * sin_z
    as_bf16 = lambda table, shape: np.asarray(table.reshape(shape), dtype=jnp.bfloat16)
    return (
        as_bf16(np.concatenate([forward_y, forward_z], axis=0), (192, 128)),
        as_bf16(forward_x, (256, 512)),
        as_bf16(inverse_x, (512, 256)),
        as_bf16(inverse_y, (1024, 512)),
        as_bf16(inverse_z, (256, 512)),
    )


def dot(a, b):
    return jnp.dot(a, b, preferred_element_type=F32)


def dot_nt(a, b):
    return lax.dot_general(a, b, (((1,), (1,)), ((), ())), preferred_element_type=F32)


def hat(spots, position):
    return jnp.maximum(1.0 - jnp.abs(spots - position), 0.0)


def iota(shape, dim):
    return lax.broadcasted_iota(jnp.int32, shape, dim)


def each_slab(me, act):
    act(lax.rem(me + 32, SLABS))

    def pair(k, carry):
        act(lax.rem(me + 32 + k, SLABS))
        act(lax.rem(me + 32 - k, SLABS))
        return carry

    lax.fori_loop(1, 32, pair, 0)


def exchange(src, dst, send_sem, recv_sem, me, chan, pick=lambda src, to: src.at[to]):
    def send(to):
        pltpu.make_async_remote_copy(
            src_ref=pick(src, to),
            dst_ref=dst.at[me],
            send_sem=send_sem,
            recv_sem=recv_sem,
            device_id=(to, chan),
            device_id_type=MESH,
        ).start()

    each_slab(me, send)


def all_but_one(dst, send_sem, recv_sem, me, chan):
    return pltpu.make_async_remote_copy(
        src_ref=dst.at[pl.ds(0, SLABS - 1)],
        dst_ref=dst.at[pl.ds(0, SLABS - 1)],
        send_sem=send_sem,
        recv_sem=recv_sem,
        device_id=(me, chan),
        device_id_type=MESH,
    )


def kernel(
    feats_in, coords_in, counts_in, lift_in, weight, skip_in, bias_in, head_in,
    fwd_yz_in, fwd_x_in, inv_x_in, inv_y_in, inv_z_in,
    out,
    feats, coords, counts, lift, skip, bias, head,
    fwd_yz, fwd_x, inv_x, inv_y, inv_z,
    a_send, a_recv, t_ref, points, embeds, packet, along,
    hat_y, hat_z, lhs, rhs, lhs_prior, rhs_prior, stage, c_send, c_recv,
    raw, packed, d_recv, acc, e_send, e_recv, skipped, spectral,
    hn, heads, back, h_send, h_recv, sums,
    load_sem, a_sem, c_sem, e_sem, h_sem, m_send, m_recv, d_send, d_rsem, g_send, g_recv,
):
    me = lax.axis_index("slab")
    chan = lax.axis_index("chan")

    loads = {}
    for k, (name, src, dst) in enumerate((
        ("feats", feats_in, feats), ("coords", coords_in, coords), ("counts", counts_in, counts),
        ("lift", lift_in, lift), ("fwd_yz", fwd_yz_in, fwd_yz), ("skip", skip_in, skip),
        ("weight", weight, raw), ("fwd_x", fwd_x_in, fwd_x), ("inv_x", inv_x_in, inv_x),
        ("inv_y", inv_y_in, inv_y), ("inv_z", inv_z_in, inv_z), ("bias", bias_in, bias),
        ("head", head_in, head),
    )):
        loads[name] = pltpu.make_async_copy(src, dst, load_sem.at[k])

    barrier = pltpu.get_barrier_semaphore()

    def greet(to):
        pl.semaphore_signal(barrier, inc=1, device_id=(to, chan), device_id_type=MESH)

    each_slab(me, greet)
    for k in range(1, CHANS):
        pl.semaphore_signal(
            barrier, inc=1, device_id=(me, lax.rem(chan + k, CHANS)), device_id_type=MESH
        )
    for load in loads.values():
        load.start()
    pending = []
    for name in ("feats", "coords", "counts", "lift"):
        loads[name].wait()

    lane = iota((16, POINTS), 1)
    mask = jnp.where((lane & 15) == iota((16, POINTS), 0), 1.0, 0.0)
    pick = jnp.where((iota((SLABS, POINTS), 1) >> 4) == iota((SLABS, POINTS), 0), 1.0, 0.0).astype(BF16)
    embed = dot(lift[...], feats[...]).astype(BF16).astype(F32)
    spot = coords[...]
    cell = (spot >> 4).astype(F32)
    part = (spot & 15).astype(F32)
    rows = [embed[v : v + 1] for v in range(8)]
    rows += [cell[v : v + 1] for v in range(3)] + [part[v : v + 1] for v in range(3)]
    spread = [(row * mask).astype(BF16) for row in rows]
    spread += [jnp.zeros((32, POINTS), BF16)]
    sorted_ = dot_nt(pick, jnp.concatenate(spread, axis=0))
    wide = jnp.broadcast_to(counts[...].astype(F32), (SLABS, SLABS))
    here = jnp.sum(jnp.where(iota((SLABS, SLABS), 0) == iota((SLABS, SLABS), 1), wide, 0.0), axis=1, keepdims=True)
    live = (iota((SLABS, 128), 1) & 15).astype(F32) < here
    a_send[0:1, 0:1, :] = jnp.zeros((1, 1, 128), F32)
    a_send[0:1, 1:2, :] = jnp.full((1, 1, 128), -8.0, F32)
    a_send[1 : SLABS + 1, 0:1, :] = jnp.where(live, sorted_[:, :128], 0.0).reshape(SLABS, 1, 128)
    a_send[1 : SLABS + 1, 1:2, :] = sorted_[:, 128:].reshape(SLABS, 1, 128)

    pl.semaphore_wait(barrier, SLABS - 1 + CHANS - 1)
    exchange(
        a_send, a_recv, a_sem.at[0], a_sem.at[1], me, chan,
        lambda src, to: src.at[pl.ds(to, 2)],
    )
    a_recv[pl.ds(me, 1)] = a_send[pl.ds(me, 2)].reshape(1, 2, 2, 128)
    a_all = all_but_one(a_recv, a_sem.at[0], a_sem.at[1], me, chan)
    pending.append(a_all)
    a_all.wait_recv()

    low = iota((8, 128), 1) < 64
    for which in range(2):
        got = a_recv[:, 1 - which]
        t_ref[which] = jnp.concatenate(
            [got[:, 0:1, :].reshape(SLABS, 128), got[:, 1:2, :].reshape(SLABS, 128)], axis=0
        ).T
        for k in range(8):
            first = t_ref[which, pl.ds(k, 8, stride=16), :]
            second = t_ref[which, pl.ds(k + 8, 8, stride=16), :]
            values = jnp.where(low, first, pltpu.roll(second, 64, 1))
            places = jnp.where(low, pltpu.roll(first, 64, 1), second)
            lanes = pl.ds(k * 128, 128)
            points[which, 0:8, lanes] = values
            points[which, 8:11, lanes] = places[0:3] + (places[3:6] + 0.5) * 0.0625
    embeds[pl.ds(chan, 1)] = points[:, 0:8, :].reshape(1, 2, 8, POINTS)

    def share(k, owner, to):
        return pltpu.make_async_remote_copy(
            src_ref=points.at[:, 0:8],
            dst_ref=embeds.at[owner],
            send_sem=m_send.at[k],
            recv_sem=m_recv.at[k],
            device_id=(me, to),
            device_id_type=MESH,
        )

    for k in range(1, CHANS):
        share(k, chan, lax.rem(chan + k, CHANS)).start()
        pending.append(share(k, chan, chan))

    loads["fwd_yz"].wait()
    base = (me * 2).astype(F32)
    down = iota((128, POINTS), 0).astype(F32)

    def transform(which, lhs, rhs):
        lanes = slice(which * POINTS, (which + 1) * POINTS)
        real_lanes, imag_lanes = slice(0, POINTS), slice(POINTS, 2 * POINTS)
        hat_y[:, lanes] = hat(down, points[which, 9:10, :]).astype(BF16)
        hat_z[:, lanes] = hat(down, points[which, 10:11, :]).astype(BF16)
        line_y = dot(fwd_yz[0:128, :], hat_y[:, lanes])
        line_z = dot(fwd_yz[128:192, :], hat_z[:, lanes])
        local = points[which, 8:9, :] - base
        planes = 2 - which
        for plane in range(planes):
            near = hat(float(plane), local)
            along[plane : plane + 1, lanes] = near
            real = (line_y[0:64] * near).astype(BF16)
            imag = (line_y[64:128] * near).astype(BF16)
            top = slice(plane * 64, plane * 64 + 64)
            low = slice((planes + plane) * 64, (planes + plane) * 64 + 64)
            lhs[top, real_lanes] = real
            lhs[top, imag_lanes] = -imag
            lhs[low, real_lanes] = imag
            lhs[low, imag_lanes] = real
        for c in range(8):
            row = points[which, c : c + 1, :]
            rhs[c * 32 : c * 32 + 32, real_lanes] = (line_z[0:32] * row).astype(BF16)
            rhs[c * 32 : c * 32 + 32, imag_lanes] = (line_z[32:64] * row).astype(BF16)
        result = dot_nt(lhs[...], rhs[...])
        for part_ in range(2):
            for plane in range(planes):
                for half in range(2):
                    rows = pl.ds(half * 4 + plane * 2 + part_, 64, stride=8)
                    at = (part_ * planes + plane) * 64
                    piece = result[at : at + 64, half * 128 : half * 128 + 128]
                    stage[rows, :] = stage[rows, :] + piece if which else piece

    transform(0, lhs, rhs)
    transform(1, lhs_prior, rhs_prior)
    c_send[...] = stage[...].reshape(SLABS, 8, 128).astype(BF16)
    exchange(c_send, c_recv, c_sem.at[0], c_sem.at[1], me, chan)
    c_recv[pl.ds(me, 1)] = c_send[pl.ds(me, 1)]
    c_all = all_but_one(c_recv, c_sem.at[0], c_sem.at[1], me, chan)
    pending.append(c_all)

    loads["weight"].wait()

    def pack(step, carry):
        kind = step // 16
        rest = step % 16
        source = (rest // 4) * 8 + rest % 4
        one = raw[kind, source]
        two = raw[kind, source + 4]
        packed[kind, rest] = jnp.concatenate([one, two], axis=-1)
        return carry

    lax.fori_loop(0, 32, pack, 0)

    for k in range(1, CHANS):
        share(k, lax.rem(chan + CHANS - k, CHANS), chan).wait_recv()
    loads["skip"].wait()
    for which in range(2):
        packet[which] = dot(skip[...], embeds[:, which].reshape(32, POINTS).astype(BF16))
    loads["bias"].wait()

    def spread(row, plane, which):
        lanes = slice(which * POINTS, (which + 1) * POINTS)
        values = hat_y[:, lanes].astype(F32) * (row * along[plane : plane + 1, lanes])
        high = values.astype(BF16)
        return high, (values - high.astype(F32)).astype(BF16)

    def deposit_own(o, carry):
        row = packet[0, pl.ds(o, 1), :]
        pieces = [*spread(row, 0, 0), *spread(row, 1, 0)]
        sums_z = dot_nt(jnp.concatenate(pieces, axis=0), hat_z[:, 0:POINTS])
        skipped[o, :, 0:128] = sums_z[0:128] + sums_z[128:256] + bias[o]
        skipped[o, :, 128:256] = sums_z[256:384] + sums_z[384:512] + bias[o]
        return carry

    lax.fori_loop(0, DEPOSIT_C, deposit_own, 0)
    c_all.wait_recv()

    loads["fwd_x"].wait()
    modes = dot(fwd_x[...], c_recv[...].astype(F32).reshape(512, 128).astype(BF16))
    turned = jnp.concatenate([modes[0:128].T, modes[128:256].T], axis=0).astype(BF16)
    d_recv[pl.ds(chan, 1)] = turned.reshape(1, 256, 128)

    def gather(k, owner, to):
        return pltpu.make_async_remote_copy(
            src_ref=d_recv.at[owner],
            dst_ref=d_recv.at[owner],
            send_sem=d_send.at[k],
            recv_sem=d_rsem.at[k],
            device_id=(me, to),
            device_id_type=MESH,
        )

    for k in (2, 1, 3):
        gather(k, chan, lax.rem(chan + k, CHANS)).start()
        pending.append(gather(k, chan, chan))

    lax.fori_loop(DEPOSIT_C, DEPOSIT_D, deposit_own, 0)
    for k in (0, 1, 3, 2):
        owner = lax.rem(chan + CHANS - k, CHANS)
        if k:
            gather(k, owner, chan).wait_recv()
        def mix(o, carry, k=k, owner=owner):
            if k:
                real, imag = acc[0, o], acc[1, o]
            else:
                real = imag = jnp.zeros((MZ, 128), F32)
            for group in range(4):
                at = owner * 4 + group
                wr, wi = packed[0, at, o], packed[1, at, o]
                vr = d_recv[owner, group * 32 : group * 32 + 32, :].astype(F32)
                vi = d_recv[owner, 128 + group * 32 : 128 + group * 32 + 32, :].astype(F32)
                real = real + (wr * vr - wi * vi)
                imag = imag + (wr * vi + wi * vr)
            acc[0, o] = real
            acc[1, o] = imag
            return carry

        lax.fori_loop(0, 8, mix, 0)
    low = iota((MZ, 128), 1) < 64
    mixed = []
    for o in range(8):
        real, imag = acc[0, o], acc[1, o]
        real = real + pltpu.roll(real, 64, 1)
        imag = imag + pltpu.roll(imag, 64, 1)
        mixed.append(jnp.where(low, real, imag).astype(BF16))
    mixed = jnp.concatenate(
        [jnp.concatenate(mixed[0:4], axis=0), jnp.concatenate(mixed[4:8], axis=0)], axis=1
    )
    loads["inv_x"].wait()
    e_send[...] = dot_nt(inv_x[...], mixed).reshape(SLABS, 8, 128).astype(BF16)
    exchange(e_send, e_recv, e_sem.at[0], e_sem.at[1], me, chan)
    e_recv[pl.ds(me, 1)] = e_send[pl.ds(me, 1)]
    e_all = all_but_one(e_recv, e_sem.at[0], e_sem.at[1], me, chan)
    pending.append(e_all)

    lax.fori_loop(DEPOSIT_D, 8, deposit_own, 0)

    def deposit_prior(o, carry):
        high, rest = spread(packet[1, pl.ds(o, 1), :], 0, 1)
        sums_z = dot_nt(jnp.concatenate([high, rest], axis=0), hat_z[:, POINTS : 2 * POINTS])
        skipped[o, :, 0:128] = skipped[o, :, 0:128] + (sums_z[0:128] + sums_z[128:256])
        return carry

    lax.fori_loop(0, 8, deposit_prior, 0)
    e_all.wait_recv()

    loads["inv_y"].wait()
    loads["inv_z"].wait()
    lines = dot(inv_y[...], e_recv[...].astype(F32).reshape(512, 128).astype(BF16)).astype(BF16)
    for block in range(4):
        half, plane = block // 2, block % 2
        at = block * 256
        both = jnp.concatenate([lines[at : at + 128], lines[at + 128 : at + 256]], axis=1)
        result = dot(both, inv_z[...])
        for group in range(4):
            spectral[half * 4 + group, :, plane * 128 : plane * 128 + 128] = result[
                :, group * 128 : group * 128 + 128
            ]

    loads["head"].wait()
    heading = head[...].astype(F32)
    shape = (32, 256)
    scale = math.sqrt(2.0 / math.pi)

    def activate(step, carry):
        at = pl.ds(step * 32, 32)
        fields = [jnp.zeros(shape, F32) for _ in range(4)]
        for o in range(8):
            x = spectral[o, at, :] + skipped[o, at, :]
            h = 0.5 * x * (1.0 + jnp.tanh(scale * (x + 0.044715 * (x * x * x))))
            for n in range(4):
                fields[n] = fields[n] + jnp.broadcast_to(heading[n : n + 1, o : o + 1], shape) * h
        for n in range(4):
            high = fields[n].astype(BF16)
            rest = (fields[n] - high.astype(F32)).astype(BF16)
            for plane in range(2):
                z = slice(plane * 128, plane * 128 + 128)
                hn[plane, n, at, 0:128] = high[:, z]
                hn[plane, n, at, 128:256] = rest[:, z]
        return carry

    lax.fori_loop(0, 4, activate, 0)

    fields = hn[...].reshape(1024, 256)
    for block in range(8):
        lanes = pl.ds(block * 256, 256)
        planes = 2 if block < 4 else 1
        grid_z = hat_z[:, lanes]
        along_z = dot(fields[0 : planes * 512], jnp.concatenate([grid_z, grid_z], axis=0))
        grid_y = hat_y[:, lanes].astype(F32)
        for n in range(4):
            sampled = jnp.zeros((1, 256), F32)
            for plane in range(planes):
                at = plane * 512 + n * 128
                line = jnp.sum(along_z[at : at + 128] * grid_y, axis=0, keepdims=True)
                sampled = sampled + line * along[plane : plane + 1, lanes]
            which = block // 4
            heads[which * 4 + n : which * 4 + n + 1, pl.ds((block % 4) * 256, 256)] = sampled
    for k in range(8):
        piece = heads[:, k * 128 : k * 128 + 128]
        back[pl.ds(k, 8, stride=16), :] = piece
        back[pl.ds(k + 8, 8, stride=16), :] = pltpu.roll(piece, 64, 1)
    h_send[...] = back[...].T[0:SLABS].reshape(SLABS, 1, 128)
    exchange(h_send, h_recv, h_sem.at[0], h_sem.at[1], me, chan)
    h_recv[pl.ds(me, 1)] = h_send[pl.ds(me, 1)]
    h_all = all_but_one(h_recv, h_sem.at[0], h_sem.at[1], me, chan)
    pending.append(h_all)
    h_all.wait_recv()

    home = h_recv[...].reshape(SLABS, 128)
    home = home + pltpu.roll(pltpu.roll(home, SLABS - 1, 0), 64, 1)
    narrow = iota((32, 128), 1) < 64
    sums[pl.ds(chan, 1)] = jnp.where(narrow, home[0:32], pltpu.roll(home[32:64], 64, 1)).reshape(1, 32, 128)

    def total(k, owner, to):
        return pltpu.make_async_remote_copy(
            src_ref=sums.at[owner],
            dst_ref=sums.at[owner],
            send_sem=g_send.at[k],
            recv_sem=g_recv.at[k],
            device_id=(me, to),
            device_id_type=MESH,
        )

    for k in range(1, CHANS):
        total(k, chan, lax.rem(chan + k, CHANS)).start()
        pending.append(total(k, chan, chan))
    pick2 = jnp.where((iota((SLABS, POINTS), 1) >> 4) == iota((SLABS, POINTS), 0), 1.0, 0.0).astype(BF16)
    cover = dot(jnp.broadcast_to(counts[...].astype(F32), (8, SLABS)).astype(BF16), pick2)
    alive = (iota((4, POINTS), 1) & 15).astype(F32) < cover[0:4]
    for k in range(1, CHANS):
        total(k, lax.rem(chan + CHANS - k, CHANS), chan).wait_recv()
    home = sums[0] + sums[1] + sums[2] + sums[3]
    home = jnp.concatenate([home, pltpu.roll(home, 64, 1)], axis=0)
    turned = jnp.concatenate([home, jnp.zeros_like(home)], axis=0).T[0:SLABS, 0:SLABS]
    top = turned.astype(BF16)
    rest = turned - top.astype(F32)
    middle = rest.astype(BF16)
    bottom = (rest - middle.astype(F32)).astype(BF16)
    laid = dot(top, pick2) + dot(middle, pick2) + dot(bottom, pick2)
    for n in range(4):
        line = jnp.sum(laid[n * 16 : n * 16 + 16] * mask, axis=0, keepdims=True)
        out[n : n + 1, :] = jnp.where(alive[n : n + 1], line, 0.0)
    out[4:8, :] = jnp.where(alive, 1.0, 0.0)

    for copy in pending:
        copy.wait_send()


def local(
    point_feats, cell_coords, send_counts, lift_weight, spec_weight,
    skip_weight, spec_bias, out_weight, out_bias,
):
    weight = jnp.swapaxes(spec_weight, 4, 5).reshape(2, 32, 8, MZ, 64)
    vmem = pl.BlockSpec(memory_space=pltpu.VMEM)
    hbm = pl.BlockSpec(memory_space=pltpu.HBM)
    dma = pltpu.SemaphoreType.DMA
    scratch = [
        pltpu.VMEM((32, POINTS), BF16),
        pltpu.VMEM((3, POINTS), jnp.int32),
        pltpu.VMEM((1, SLABS), jnp.int32),
        pltpu.VMEM((8, 32), BF16),
        pltpu.VMEM((8, 32), BF16),
        pltpu.SMEM((8,), F32),
        pltpu.VMEM((4, 8), BF16),
        pltpu.VMEM((192, 128), BF16),
        pltpu.VMEM((256, 512), BF16),
        pltpu.VMEM((512, 256), BF16),
        pltpu.VMEM((1024, 512), BF16),
        pltpu.VMEM((256, 512), BF16),
        pltpu.VMEM((SLABS + 1, 2, 128), F32),
        pltpu.VMEM((SLABS, 2, 2, 128), F32),
        pltpu.VMEM((2, 128, 128), F32),
        pltpu.VMEM((2, 16, POINTS), F32),
        pltpu.VMEM((CHANS, 2, 8, POINTS), F32),
        pltpu.VMEM((2, 8, POINTS), F32),
        pltpu.VMEM((8, 2 * POINTS), F32),
        pltpu.VMEM((128, 2 * POINTS), BF16),
        pltpu.VMEM((128, 2 * POINTS), BF16),
        pltpu.VMEM((256, 2 * POINTS), BF16),
        pltpu.VMEM((256, 2 * POINTS), BF16),
        pltpu.VMEM((128, 2 * POINTS), BF16),
        pltpu.VMEM((256, 2 * POINTS), BF16),
        pltpu.VMEM((512, 128), F32),
        pltpu.VMEM((SLABS, 8, 128), BF16),
        pltpu.VMEM((SLABS, 8, 128), BF16),
        pltpu.VMEM((2, 32, 8, MZ, 64), F32),
        pltpu.VMEM((2, 16, 8, MZ, 128), F32),
        pltpu.VMEM((CHANS, 256, 128), BF16),
        pltpu.VMEM((2, 8, MZ, 128), F32),
        pltpu.VMEM((SLABS, 8, 128), BF16),
        pltpu.VMEM((SLABS, 8, 128), BF16),
        pltpu.VMEM((8, 128, 256), F32),
        pltpu.VMEM((8, 128, 256), F32),
        pltpu.VMEM((2, 4, 128, 256), BF16),
        pltpu.VMEM((8, POINTS), F32),
        pltpu.VMEM((128, 128), F32),
        pltpu.VMEM((SLABS, 1, 128), F32),
        pltpu.VMEM((SLABS, 1, 128), F32),
        pltpu.VMEM((CHANS, 32, 128), F32),
        dma((13,)),
        dma((2,)),
        dma((2,)),
        dma((2,)),
        dma((2,)),
        dma((CHANS,)),
        dma((CHANS,)),
        dma((CHANS,)),
        dma((CHANS,)),
        dma((CHANS,)),
        dma((CHANS,)),
    ]
    result = pl.pallas_call(
        kernel,
        out_shape=jax.ShapeDtypeStruct((8, POINTS), F32),
        in_specs=[hbm] * 13,
        out_specs=vmem,
        scratch_shapes=scratch,
        compiler_params=pltpu.CompilerParams(
            collective_id=0, has_side_effects=True, vmem_limit_bytes=60 * 1024 * 1024
        ),
    )(
        point_feats, cell_coords, send_counts, lift_weight.T, weight,
        skip_weight.T, spec_bias, out_weight.T, *(jnp.asarray(t) for t in tables()),
    )
    return result[0:4] + out_bias[:, None] * result[4:8]


def solution(mesh):
    in_specs = (
        P(None, "slab"),
        P(None, "slab"),
        P("slab", None),
        P(None, "chan"),
        P(None, None, "chan", "slab", None, None),
        P(None, "chan"),
        P("chan"),
        P("chan", None),
        P(),
    )
    out_specs = P(None, "slab")
    return jax.shard_map(local, mesh=mesh, in_specs=in_specs, out_specs=out_specs, check_vma=False)
```

```python
import functools
import math

import jax
import jax.numpy as jnp
import numpy as np
from jax import lax
from jax.experimental import pallas as pl
from jax.experimental.pallas import tpu as pltpu
from jax.sharding import PartitionSpec as P

GRID = 128
MZ = 32
CAP = 16
SLABS = 64
CHANS = 4
POINTS = 1024
DEPOSIT_C = 3
DEPOSIT_D = 4
MODES = np.concatenate([np.arange(MZ), np.arange(GRID - MZ, GRID)])
MESH = pl.DeviceIdType.MESH
F32 = jnp.float32
BF16 = jnp.bfloat16


def wave(freqs, positions):
    angle = (freqs[:, None] * positions[None, :] % GRID) * (2.0 * math.pi / GRID)
    return np.cos(angle), np.sin(angle)


def tables():
    spots = np.arange(GRID)
    cos_y, sin_y = wave(MODES, spots)
    cos_z, sin_z = wave(np.arange(MZ), spots)
    forward_y = np.concatenate([cos_y, -sin_y], axis=0)
    forward_z = np.concatenate([cos_z, -sin_z], axis=0)
    planes = np.arange(SLABS)[:, None] * 2 + np.arange(2)[None, :]
    cos_x, sin_x = wave(MODES, planes.reshape(-1) % GRID)
    cos_x = cos_x.reshape(64, SLABS, 2)
    sin_x = sin_x.reshape(64, SLABS, 2)
    forward_x = np.zeros((2, 2, 64, SLABS, 2, 2, 2))
    inverse_x = np.zeros((SLABS, 2, 2, 2, 2, 2, 64))
    for half in range(2):
        for plane in range(2):
            c, s = cos_x[:, :, plane], sin_x[:, :, plane]
            forward_x[0, half, :, :, half, plane, 0] = c
            forward_x[0, half, :, :, half, plane, 1] = s
            forward_x[1, half, :, :, half, plane, 0] = -s
            forward_x[1, half, :, :, half, plane, 1] = c
            inverse_x[:, half, plane, 0, half, 0] = c.T
            inverse_x[:, half, plane, 0, half, 1] = -s.T
            inverse_x[:, half, plane, 1, half, 0] = s.T
            inverse_x[:, half, plane, 1, half, 1] = c.T
    inverse_y = np.zeros((4, 2, GRID, 64, 4, 2))
    for block in range(4):
        inverse_y[block, 0, :, :, block, 0] = cos_y.T
        inverse_y[block, 0, :, :, block, 1] = -sin_y.T
        inverse_y[block, 1, :, :, block, 0] = sin_y.T
        inverse_y[block, 1, :, :, block, 1] = cos_y.T
    factor = np.where(np.arange(MZ) == 0, 1.0, 2.0)[:, None] / float(GRID) ** 3
    inverse_z = np.zeros((2, 4, MZ, 4, GRID))
    for group in range(4):
        inverse_z[0, group, :, group] = factor * cos_z
        inverse_z[1, group, :, group] = -factor * sin_z
    as_bf16 = lambda table, shape: np.asarray(table.reshape(shape), dtype=jnp.bfloat16)
    return (
        as_bf16(np.concatenate([forward_y, forward_z], axis=0), (192, 128)),
        as_bf16(forward_x, (256, 512)),
        as_bf16(inverse_x, (512, 256)),
        as_bf16(inverse_y, (1024, 512)),
        as_bf16(inverse_z, (256, 512)),
    )


def dot(a, b):
    return jnp.dot(a, b, preferred_element_type=F32)


def dot_nt(a, b):
    return lax.dot_general(a, b, (((1,), (1,)), ((), ())), preferred_element_type=F32)


def hat(spots, position):
    return jnp.maximum(1.0 - jnp.abs(spots - position), 0.0)


def iota(shape, dim):
    return lax.broadcasted_iota(jnp.int32, shape, dim)


def each_slab(me, act):
    act(lax.rem(me + 32, SLABS))

    def pair(k, carry):
        act(lax.rem(me + 32 + k, SLABS))
        act(lax.rem(me + 32 - k, SLABS))
        return carry

    lax.fori_loop(1, 32, pair, 0)


def exchange(src, dst, send_sem, recv_sem, me, chan, pick=lambda src, to: src.at[to]):
    def send(to):
        pltpu.make_async_remote_copy(
            src_ref=pick(src, to),
            dst_ref=dst.at[me],
            send_sem=send_sem,
            recv_sem=recv_sem,
            device_id=(to, chan),
            device_id_type=MESH,
        ).start()

    each_slab(me, send)


def all_but_one(dst, send_sem, recv_sem, me, chan):
    return pltpu.make_async_remote_copy(
        src_ref=dst.at[pl.ds(0, SLABS - 1)],
        dst_ref=dst.at[pl.ds(0, SLABS - 1)],
        send_sem=send_sem,
        recv_sem=recv_sem,
        device_id=(me, chan),
        device_id_type=MESH,
    )


def kernel(
    feats_in, coords_in, counts_in, lift_in, weight, skip_in, bias_in, head_in,
    fwd_yz_in, fwd_x_in, inv_x_in, inv_y_in, inv_z_in,
    out,
    feats, coords, counts, lift, skip, bias, head,
    fwd_yz, fwd_x, inv_x, inv_y, inv_z,
    a_send, a_recv, t_ref, points, embeds, packet, along,
    hat_y, hat_z, lhs, rhs, lhs_prior, rhs_prior, stage, c_send, c_recv,
    raw, packed, d_recv, acc, e_send, e_recv, skipped, spectral,
    hn, heads, back, h_send, h_recv, sums,
    load_sem, a_sem, c_sem, e_sem, h_sem, m_send, m_recv, d_send, d_rsem, g_send, g_recv,
):
    me = lax.axis_index("slab")
    chan = lax.axis_index("chan")

    loads = {}
    for k, (name, src, dst) in enumerate((
        ("feats", feats_in, feats), ("coords", coords_in, coords), ("counts", counts_in, counts),
        ("lift", lift_in, lift), ("fwd_yz", fwd_yz_in, fwd_yz), ("skip", skip_in, skip),
        ("weight", weight, raw), ("fwd_x", fwd_x_in, fwd_x), ("inv_x", inv_x_in, inv_x),
        ("inv_y", inv_y_in, inv_y), ("inv_z", inv_z_in, inv_z), ("bias", bias_in, bias),
        ("head", head_in, head),
    )):
        loads[name] = pltpu.make_async_copy(src, dst, load_sem.at[k])

    barrier = pltpu.get_barrier_semaphore()

    def greet(to):
        pl.semaphore_signal(barrier, inc=1, device_id=(to, chan), device_id_type=MESH)

    each_slab(me, greet)
    for k in range(1, CHANS):
        pl.semaphore_signal(
            barrier, inc=1, device_id=(me, lax.rem(chan + k, CHANS)), device_id_type=MESH
        )
    for load in loads.values():
        load.start()
    pending = []
    for name in ("feats", "coords", "counts", "lift"):
        loads[name].wait()

    lane = iota((16, POINTS), 1)
    mask = jnp.where((lane & 15) == iota((16, POINTS), 0), 1.0, 0.0)
    pick = jnp.where((iota((SLABS, POINTS), 1) >> 4) == iota((SLABS, POINTS), 0), 1.0, 0.0).astype(BF16)
    embed = dot(lift[...], feats[...]).astype(BF16).astype(F32)
    spot = coords[...]
    cell = (spot >> 4).astype(F32)
    part = (spot & 15).astype(F32)
    rows = [embed[v : v + 1] for v in range(8)]
    rows += [cell[v : v + 1] for v in range(3)] + [part[v : v + 1] for v in range(3)]
    spread = [(row * mask).astype(BF16) for row in rows]
    spread += [jnp.zeros((32, POINTS), BF16)]
    sorted_ = dot_nt(pick, jnp.concatenate(spread, axis=0))
    wide = jnp.broadcast_to(counts[...].astype(F32), (SLABS, SLABS))
    here = jnp.sum(jnp.where(iota((SLABS, SLABS), 0) == iota((SLABS, SLABS), 1), wide, 0.0), axis=1, keepdims=True)
    live = (iota((SLABS, 128), 1) & 15).astype(F32) < here
    a_send[0:1, 0:1, :] = jnp.zeros((1, 1, 128), F32)
    a_send[0:1, 1:2, :] = jnp.full((1, 1, 128), -8.0, F32)
    a_send[1 : SLABS + 1, 0:1, :] = jnp.where(live, sorted_[:, :128], 0.0).reshape(SLABS, 1, 128)
    a_send[1 : SLABS + 1, 1:2, :] = sorted_[:, 128:].reshape(SLABS, 1, 128)

    pl.semaphore_wait(barrier, SLABS - 1 + CHANS - 1)
    exchange(
        a_send, a_recv, a_sem.at[0], a_sem.at[1], me, chan,
        lambda src, to: src.at[pl.ds(to, 2)],
    )
    a_recv[pl.ds(me, 1)] = a_send[pl.ds(me, 2)].reshape(1, 2, 2, 128)
    a_all = all_but_one(a_recv, a_sem.at[0], a_sem.at[1], me, chan)
    pending.append(a_all)
    a_all.wait_recv()

    low = iota((8, 128), 1) < 64
    for which in range(2):
        got = a_recv[:, 1 - which]
        t_ref[which] = jnp.concatenate(
            [got[:, 0:1, :].reshape(SLABS, 128), got[:, 1:2, :].reshape(SLABS, 128)], axis=0
        ).T
        for k in range(8):
            first = t_ref[which, pl.ds(k, 8, stride=16), :]
            second = t_ref[which, pl.ds(k + 8, 8, stride=16), :]
            values = jnp.where(low, first, pltpu.roll(second, 64, 1))
            places = jnp.where(low, pltpu.roll(first, 64, 1), second)
            lanes = pl.ds(k * 128, 128)
            points[which, 0:8, lanes] = values
            points[which, 8:11, lanes] = places[0:3] + (places[3:6] + 0.5) * 0.0625
    embeds[pl.ds(chan, 1)] = points[:, 0:8, :].reshape(1, 2, 8, POINTS)

    def share(k, owner, to):
        return pltpu.make_async_remote_copy(
            src_ref=points.at[:, 0:8],
            dst_ref=embeds.at[owner],
            send_sem=m_send.at[k],
            recv_sem=m_recv.at[k],
            device_id=(me, to),
            device_id_type=MESH,
        )

    for k in (1, 3, 2):
        share(k, chan, lax.rem(chan + k, CHANS)).start()
        pending.append(share(k, chan, chan))

    loads["fwd_yz"].wait()
    base = (me * 2).astype(F32)
    down = iota((128, POINTS), 0).astype(F32)

    def transform(which, lhs, rhs):
        lanes = slice(which * POINTS, (which + 1) * POINTS)
        real_lanes, imag_lanes = slice(0, POINTS), slice(POINTS, 2 * POINTS)
        hat_y[:, lanes] = hat(down, points[which, 9:10, :]).astype(BF16)
        hat_z[:, lanes] = hat(down, points[which, 10:11, :]).astype(BF16)
        line_y = dot(fwd_yz[0:128, :], hat_y[:, lanes])
        line_z = dot(fwd_yz[128:192, :], hat_z[:, lanes])
        local = points[which, 8:9, :] - base
        planes = 2 - which
        for plane in range(planes):
            near = hat(float(plane), local)
            along[plane : plane + 1, lanes] = near
            real = (line_y[0:64] * near).astype(BF16)
            imag = (line_y[64:128] * near).astype(BF16)
            top = slice(plane * 64, plane * 64 + 64)
            low = slice((planes + plane) * 64, (planes + plane) * 64 + 64)
            lhs[top, real_lanes] = real
            lhs[top, imag_lanes] = -imag
            lhs[low, real_lanes] = imag
            lhs[low, imag_lanes] = real
        for c in range(8):
            row = points[which, c : c + 1, :]
            rhs[c * 32 : c * 32 + 32, real_lanes] = (line_z[0:32] * row).astype(BF16)
            rhs[c * 32 : c * 32 + 32, imag_lanes] = (line_z[32:64] * row).astype(BF16)
        result = dot_nt(lhs[...], rhs[...])
        for part_ in range(2):
            for plane in range(planes):
                for half in range(2):
                    rows = pl.ds(half * 4 + plane * 2 + part_, 64, stride=8)
                    at = (part_ * planes + plane) * 64
                    piece = result[at : at + 64, half * 128 : half * 128 + 128]
                    stage[rows, :] = stage[rows, :] + piece if which else piece

    transform(0, lhs, rhs)
    transform(1, lhs_prior, rhs_prior)
    c_send[...] = stage[...].reshape(SLABS, 8, 128).astype(BF16)
    exchange(c_send, c_recv, c_sem.at[0], c_sem.at[1], me, chan)
    c_recv[pl.ds(me, 1)] = c_send[pl.ds(me, 1)]
    c_all = all_but_one(c_recv, c_sem.at[0], c_sem.at[1], me, chan)
    pending.append(c_all)

    loads["weight"].wait()

    def pack(step, carry):
        kind = step // 16
        rest = step % 16
        source = (rest // 4) * 8 + rest % 4
        one = raw[kind, source]
        two = raw[kind, source + 4]
        packed[kind, rest] = jnp.concatenate([one, two], axis=-1)
        return carry

    lax.fori_loop(0, 32, pack, 0)

    for k in range(1, CHANS):
        share(k, lax.rem(chan + CHANS - k, CHANS), chan).wait_recv()
    loads["skip"].wait()
    for which in range(2):
        packet[which] = dot(skip[...], embeds[:, which].reshape(32, POINTS).astype(BF16))
    loads["bias"].wait()

    def spread(row, plane, which):
        lanes = slice(which * POINTS, (which + 1) * POINTS)
        values = hat_y[:, lanes].astype(F32) * (row * along[plane : plane + 1, lanes])
        high = values.astype(BF16)
        return high, (values - high.astype(F32)).astype(BF16)

    def deposit_own(o, carry):
        row = packet[0, pl.ds(o, 1), :]
        pieces = [*spread(row, 0, 0), *spread(row, 1, 0)]
        sums_z = dot_nt(jnp.concatenate(pieces, axis=0), hat_z[:, 0:POINTS])
        skipped[o, :, 0:128] = sums_z[0:128] + sums_z[128:256] + bias[o]
        skipped[o, :, 128:256] = sums_z[256:384] + sums_z[384:512] + bias[o]
        return carry

    lax.fori_loop(0, DEPOSIT_C, deposit_own, 0)
    c_all.wait_recv()

    loads["fwd_x"].wait()
    modes = dot(fwd_x[...], c_recv[...].astype(F32).reshape(512, 128).astype(BF16))
    turned = jnp.concatenate([modes[0:128].T, modes[128:256].T], axis=0).astype(BF16)
    d_recv[pl.ds(chan, 1)] = turned.reshape(1, 256, 128)

    def gather(k, owner, to):
        return pltpu.make_async_remote_copy(
            src_ref=d_recv.at[owner],
            dst_ref=d_recv.at[owner],
            send_sem=d_send.at[k],
            recv_sem=d_rsem.at[k],
            device_id=(me, to),
            device_id_type=MESH,
        )

    for k in (1, 3, 2):
        gather(k, chan, lax.rem(chan + k, CHANS)).start()
        pending.append(gather(k, chan, chan))

    lax.fori_loop(DEPOSIT_C, DEPOSIT_D, deposit_own, 0)
    for k in (0, 1, 3, 2):
        owner = lax.rem(chan + CHANS - k, CHANS)
        if k:
            gather(k, owner, chan).wait_recv()
        def mix(o, carry, k=k, owner=owner):
            if k:
                real, imag = acc[0, o], acc[1, o]
            else:
                real = imag = jnp.zeros((MZ, 128), F32)
            for group in range(4):
                at = owner * 4 + group
                wr, wi = packed[0, at, o], packed[1, at, o]
                vr = d_recv[owner, group * 32 : group * 32 + 32, :].astype(F32)
                vi = d_recv[owner, 128 + group * 32 : 128 + group * 32 + 32, :].astype(F32)
                real = real + (wr * vr - wi * vi)
                imag = imag + (wr * vi + wi * vr)
            acc[0, o] = real
            acc[1, o] = imag
            return carry

        lax.fori_loop(0, 8, mix, 0)
    low = iota((MZ, 128), 1) < 64
    mixed = []
    for o in range(8):
        real, imag = acc[0, o], acc[1, o]
        real = real + pltpu.roll(real, 64, 1)
        imag = imag + pltpu.roll(imag, 64, 1)
        mixed.append(jnp.where(low, real, imag).astype(BF16))
    mixed = jnp.concatenate(
        [jnp.concatenate(mixed[0:4], axis=0), jnp.concatenate(mixed[4:8], axis=0)], axis=1
    )
    loads["inv_x"].wait()
    e_send[...] = dot_nt(inv_x[...], mixed).reshape(SLABS, 8, 128).astype(BF16)
    exchange(e_send, e_recv, e_sem.at[0], e_sem.at[1], me, chan)
    e_recv[pl.ds(me, 1)] = e_send[pl.ds(me, 1)]
    e_all = all_but_one(e_recv, e_sem.at[0], e_sem.at[1], me, chan)
    pending.append(e_all)

    lax.fori_loop(DEPOSIT_D, 8, deposit_own, 0)

    def deposit_prior(o, carry):
        high, rest = spread(packet[1, pl.ds(o, 1), :], 0, 1)
        sums_z = dot_nt(jnp.concatenate([high, rest], axis=0), hat_z[:, POINTS : 2 * POINTS])
        skipped[o, :, 0:128] = skipped[o, :, 0:128] + (sums_z[0:128] + sums_z[128:256])
        return carry

    lax.fori_loop(0, 8, deposit_prior, 0)
    e_all.wait_recv()

    loads["inv_y"].wait()
    loads["inv_z"].wait()
    lines = dot(inv_y[...], e_recv[...].astype(F32).reshape(512, 128).astype(BF16)).astype(BF16)
    both = [
        jnp.concatenate([lines[at : at + 128], lines[at + 128 : at + 256]], axis=1)
        for at in range(0, 1024, 256)
    ]
    result = dot(jnp.concatenate(both, axis=0), inv_z[...])
    for block in range(4):
        half, plane = block // 2, block % 2
        for group in range(4):
            spectral[half * 4 + group, :, plane * 128 : plane * 128 + 128] = result[
                block * 128 : block * 128 + 128, group * 128 : group * 128 + 128
            ]

    loads["head"].wait()
    heading = 0.5 * head[...].astype(F32)
    shape = (32, 256)
    scale = math.sqrt(2.0 / math.pi)

    def activate(step, carry):
        at = pl.ds(step * 32, 32)
        fields = [jnp.zeros(shape, F32) for _ in range(4)]
        for o in range(8):
            x = spectral[o, at, :] + skipped[o, at, :]
            h = x + x * jnp.tanh(x * (scale + (scale * 0.044715) * (x * x)))
            for n in range(4):
                fields[n] = fields[n] + jnp.broadcast_to(heading[n : n + 1, o : o + 1], shape) * h
        for n in range(4):
            high = fields[n].astype(BF16)
            rest = (fields[n] - high.astype(F32)).astype(BF16)
            for plane in range(2):
                z = slice(plane * 128, plane * 128 + 128)
                hn[plane, n, at, 0:128] = high[:, z]
                hn[plane, n, at, 128:256] = rest[:, z]
        return carry

    lax.fori_loop(0, 4, activate, 0)

    fields = hn[...].reshape(1024, 256)
    for block in range(8):
        lanes = pl.ds(block * 256, 256)
        planes = 2 if block < 4 else 1
        grid_z = hat_z[:, lanes]
        along_z = dot(fields[0 : planes * 512], jnp.concatenate([grid_z, grid_z], axis=0))
        grid_y = hat_y[:, lanes].astype(F32)
        for n in range(4):
            sampled = jnp.zeros((1, 256), F32)
            for plane in range(planes):
                at = plane * 512 + n * 128
                line = jnp.sum(along_z[at : at + 128] * grid_y, axis=0, keepdims=True)
                sampled = sampled + line * along[plane : plane + 1, lanes]
            which = block // 4
            heads[which * 4 + n : which * 4 + n + 1, pl.ds((block % 4) * 256, 256)] = sampled
    for k in range(8):
        piece = heads[:, k * 128 : k * 128 + 128]
        back[pl.ds(k, 8, stride=16), :] = piece
        back[pl.ds(k + 8, 8, stride=16), :] = pltpu.roll(piece, 64, 1)
    h_send[...] = back[...].T[0:SLABS].reshape(SLABS, 1, 128)
    exchange(h_send, h_recv, h_sem.at[0], h_sem.at[1], me, chan)
    h_recv[pl.ds(me, 1)] = h_send[pl.ds(me, 1)]
    h_all = all_but_one(h_recv, h_sem.at[0], h_sem.at[1], me, chan)
    pending.append(h_all)
    h_all.wait_recv()

    home = h_recv[...].reshape(SLABS, 128)
    home = home + pltpu.roll(pltpu.roll(home, SLABS - 1, 0), 64, 1)
    narrow = iota((32, 128), 1) < 64
    sums[pl.ds(chan, 1)] = jnp.where(narrow, home[0:32], pltpu.roll(home[32:64], 64, 1)).reshape(1, 32, 128)

    def total(k, owner, to):
        return pltpu.make_async_remote_copy(
            src_ref=sums.at[owner],
            dst_ref=sums.at[owner],
            send_sem=g_send.at[k],
            recv_sem=g_recv.at[k],
            device_id=(me, to),
            device_id_type=MESH,
        )

    for k in (1, 3, 2):
        total(k, chan, lax.rem(chan + k, CHANS)).start()
        pending.append(total(k, chan, chan))
    pick2 = jnp.where((iota((SLABS, POINTS), 1) >> 4) == iota((SLABS, POINTS), 0), 1.0, 0.0).astype(BF16)
    cover = dot(jnp.broadcast_to(counts[...].astype(F32), (8, SLABS)).astype(BF16), pick2)
    alive = (iota((4, POINTS), 1) & 15).astype(F32) < cover[0:4]
    for k in range(1, CHANS):
        total(k, lax.rem(chan + CHANS - k, CHANS), chan).wait_recv()
    home = sums[0] + sums[1] + sums[2] + sums[3]
    home = jnp.concatenate([home, pltpu.roll(home, 64, 1)], axis=0)
    turned = jnp.concatenate([home, jnp.zeros_like(home)], axis=0).T[0:SLABS, 0:SLABS]
    top = turned.astype(BF16)
    rest = turned - top.astype(F32)
    middle = rest.astype(BF16)
    bottom = (rest - middle.astype(F32)).astype(BF16)
    laid = dot(top, pick2) + dot(middle, pick2) + dot(bottom, pick2)
    for n in range(4):
        line = jnp.sum(laid[n * 16 : n * 16 + 16] * mask, axis=0, keepdims=True)
        out[n : n + 1, :] = jnp.where(alive[n : n + 1], line, 0.0)
    out[4:8, :] = jnp.where(alive, 1.0, 0.0)

    for copy in pending:
        copy.wait_send()


def local(
    point_feats, cell_coords, send_counts, lift_weight, spec_weight,
    skip_weight, spec_bias, out_weight, out_bias,
):
    weight = jnp.swapaxes(spec_weight, 4, 5).reshape(2, 32, 8, MZ, 64)
    vmem = pl.BlockSpec(memory_space=pltpu.VMEM)
    hbm = pl.BlockSpec(memory_space=pltpu.HBM)
    dma = pltpu.SemaphoreType.DMA
    scratch = [
        pltpu.VMEM((32, POINTS), BF16),
        pltpu.VMEM((3, POINTS), jnp.int32),
        pltpu.VMEM((1, SLABS), jnp.int32),
        pltpu.VMEM((8, 32), BF16),
        pltpu.VMEM((8, 32), BF16),
        pltpu.SMEM((8,), F32),
        pltpu.VMEM((4, 8), BF16),
        pltpu.VMEM((192, 128), BF16),
        pltpu.VMEM((256, 512), BF16),
        pltpu.VMEM((512, 256), BF16),
        pltpu.VMEM((1024, 512), BF16),
        pltpu.VMEM((256, 512), BF16),
        pltpu.VMEM((SLABS + 1, 2, 128), F32),
        pltpu.VMEM((SLABS, 2, 2, 128), F32),
        pltpu.VMEM((2, 128, 128), F32),
        pltpu.VMEM((2, 16, POINTS), F32),
        pltpu.VMEM((CHANS, 2, 8, POINTS), F32),
        pltpu.VMEM((2, 8, POINTS), F32),
        pltpu.VMEM((8, 2 * POINTS), F32),
        pltpu.VMEM((128, 2 * POINTS), BF16),
        pltpu.VMEM((128, 2 * POINTS), BF16),
        pltpu.VMEM((256, 2 * POINTS), BF16),
        pltpu.VMEM((256, 2 * POINTS), BF16),
        pltpu.VMEM((128, 2 * POINTS), BF16),
        pltpu.VMEM((256, 2 * POINTS), BF16),
        pltpu.VMEM((512, 128), F32),
        pltpu.VMEM((SLABS, 8, 128), BF16),
        pltpu.VMEM((SLABS, 8, 128), BF16),
        pltpu.VMEM((2, 32, 8, MZ, 64), F32),
        pltpu.VMEM((2, 16, 8, MZ, 128), F32),
        pltpu.VMEM((CHANS, 256, 128), BF16),
        pltpu.VMEM((2, 8, MZ, 128), F32),
        pltpu.VMEM((SLABS, 8, 128), BF16),
        pltpu.VMEM((SLABS, 8, 128), BF16),
        pltpu.VMEM((8, 128, 256), F32),
        pltpu.VMEM((8, 128, 256), F32),
        pltpu.VMEM((2, 4, 128, 256), BF16),
        pltpu.VMEM((8, POINTS), F32),
        pltpu.VMEM((128, 128), F32),
        pltpu.VMEM((SLABS, 1, 128), F32),
        pltpu.VMEM((SLABS, 1, 128), F32),
        pltpu.VMEM((CHANS, 32, 128), F32),
        dma((13,)),
        dma((2,)),
        dma((2,)),
        dma((2,)),
        dma((2,)),
        dma((CHANS,)),
        dma((CHANS,)),
        dma((CHANS,)),
        dma((CHANS,)),
        dma((CHANS,)),
        dma((CHANS,)),
    ]
    result = pl.pallas_call(
        kernel,
        out_shape=jax.ShapeDtypeStruct((8, POINTS), F32),
        in_specs=[hbm] * 13,
        out_specs=vmem,
        scratch_shapes=scratch,
        compiler_params=pltpu.CompilerParams(
            collective_id=0, has_side_effects=True, vmem_limit_bytes=60 * 1024 * 1024
        ),
    )(
        point_feats, cell_coords, send_counts, lift_weight.T, weight,
        skip_weight.T, spec_bias, out_weight.T, *(jnp.asarray(t) for t in tables()),
    )
    return result[0:4] + out_bias[:, None] * result[4:8]


def solution(mesh):
    in_specs = (
        P(None, "slab"),
        P(None, "slab"),
        P("slab", None),
        P(None, "chan"),
        P(None, None, "chan", "slab", None, None),
        P(None, "chan"),
        P("chan"),
        P("chan", None),
        P(),
    )
    out_specs = P(None, "slab")
    return jax.shard_map(local, mesh=mesh, in_specs=in_specs, out_specs=out_specs, check_vma=False)
```

```python
import functools
import math

import jax
import jax.numpy as jnp
import numpy as np
from jax import lax
from jax.experimental import pallas as pl
from jax.experimental.pallas import tpu as pltpu
from jax.sharding import PartitionSpec as P

GRID = 128
MZ = 32
CAP = 16
SLABS = 64
CHANS = 4
POINTS = 1024
DEPOSIT_C = 3
DEPOSIT_D = 4
MODES = np.concatenate([np.arange(MZ), np.arange(GRID - MZ, GRID)])
MESH = pl.DeviceIdType.MESH
F32 = jnp.float32
BF16 = jnp.bfloat16


def wave(freqs, positions):
    angle = (freqs[:, None] * positions[None, :] % GRID) * (2.0 * math.pi / GRID)
    return np.cos(angle), np.sin(angle)


def tables():
    spots = np.arange(GRID)
    cos_y, sin_y = wave(MODES, spots)
    cos_z, sin_z = wave(np.arange(MZ), spots)
    forward_y = np.concatenate([cos_y, -sin_y], axis=0)
    forward_z = np.concatenate([cos_z, -sin_z], axis=0)
    planes = np.arange(SLABS)[:, None] * 2 + np.arange(2)[None, :]
    cos_x, sin_x = wave(MODES, planes.reshape(-1) % GRID)
    cos_x = cos_x.reshape(64, SLABS, 2)
    sin_x = sin_x.reshape(64, SLABS, 2)
    forward_x = np.zeros((2, 2, 64, SLABS, 2, 2, 2))
    inverse_x = np.zeros((SLABS, 2, 2, 2, 2, 2, 64))
    for half in range(2):
        for plane in range(2):
            c, s = cos_x[:, :, plane], sin_x[:, :, plane]
            forward_x[0, half, :, :, half, plane, 0] = c
            forward_x[0, half, :, :, half, plane, 1] = s
            forward_x[1, half, :, :, half, plane, 0] = -s
            forward_x[1, half, :, :, half, plane, 1] = c
            inverse_x[:, half, plane, 0, half, 0] = c.T
            inverse_x[:, half, plane, 0, half, 1] = -s.T
            inverse_x[:, half, plane, 1, half, 0] = s.T
            inverse_x[:, half, plane, 1, half, 1] = c.T
    inverse_y = np.zeros((4, 2, GRID, 64, 4, 2))
    for block in range(4):
        inverse_y[block, 0, :, :, block, 0] = cos_y.T
        inverse_y[block, 0, :, :, block, 1] = -sin_y.T
        inverse_y[block, 1, :, :, block, 0] = sin_y.T
        inverse_y[block, 1, :, :, block, 1] = cos_y.T
    factor = np.where(np.arange(MZ) == 0, 1.0, 2.0)[:, None] / float(GRID) ** 3
    inverse_z = np.zeros((2, 4, MZ, 4, GRID))
    for group in range(4):
        inverse_z[0, group, :, group] = factor * cos_z
        inverse_z[1, group, :, group] = -factor * sin_z
    as_bf16 = lambda table, shape: np.asarray(table.reshape(shape), dtype=jnp.bfloat16)
    return (
        as_bf16(np.concatenate([forward_y, forward_z], axis=0), (192, 128)),
        as_bf16(forward_x, (256, 512)),
        as_bf16(inverse_x, (512, 256)),
        as_bf16(inverse_y, (1024, 512)),
        as_bf16(inverse_z, (256, 512)),
    )


def dot(a, b):
    return jnp.dot(a, b, preferred_element_type=F32)


def dot_nt(a, b):
    return lax.dot_general(a, b, (((1,), (1,)), ((), ())), preferred_element_type=F32)


def hat(spots, position):
    return jnp.maximum(1.0 - jnp.abs(spots - position), 0.0)


def iota(shape, dim):
    return lax.broadcasted_iota(jnp.int32, shape, dim)


def each_slab(me, act):
    act(lax.rem(me + 36, SLABS))

    def pair(k, carry):
        act(lax.rem(me + 36 + k, SLABS))
        act(lax.rem(me + 36 - k, SLABS))
        return carry

    lax.fori_loop(1, 28, pair, 0)

    def near(k, carry):
        act(lax.rem(me + 8 - k, SLABS))
        return carry

    lax.fori_loop(0, 8, near, 0)


def exchange(src, dst, send_sem, recv_sem, me, chan, pick=lambda src, to: src.at[to]):
    def send(to):
        pltpu.make_async_remote_copy(
            src_ref=pick(src, to),
            dst_ref=dst.at[me],
            send_sem=send_sem,
            recv_sem=recv_sem,
            device_id=(to, chan),
            device_id_type=MESH,
        ).start()

    each_slab(me, send)


def all_but_one(dst, send_sem, recv_sem, me, chan):
    return pltpu.make_async_remote_copy(
        src_ref=dst.at[pl.ds(0, SLABS - 1)],
        dst_ref=dst.at[pl.ds(0, SLABS - 1)],
        send_sem=send_sem,
        recv_sem=recv_sem,
        device_id=(me, chan),
        device_id_type=MESH,
    )


def kernel(
    feats_in, coords_in, counts_in, lift_in, weight, skip_in, bias_in, head_in,
    fwd_yz_in, fwd_x_in, inv_x_in, inv_y_in, inv_z_in,
    out,
    feats, coords, counts, lift, skip, bias, head,
    fwd_yz, fwd_x, inv_x, inv_y, inv_z,
    a_send, a_recv, t_ref, points, embeds, packet, along,
    hat_y, hat_z, lhs, rhs, lhs_prior, rhs_prior, stage, c_send, c_recv,
    raw, packed, d_recv, acc, e_send, e_recv, skipped, spectral,
    hn, heads, back, h_send, h_recv, sums,
    load_sem, a_sem, c_sem, e_sem, h_sem, m_send, m_recv, d_send, d_rsem, g_send, g_recv,
):
    me = lax.axis_index("slab")
    chan = lax.axis_index("chan")

    loads = {}
    for k, (name, src, dst) in enumerate((
        ("feats", feats_in, feats), ("coords", coords_in, coords), ("counts", counts_in, counts),
        ("lift", lift_in, lift), ("fwd_yz", fwd_yz_in, fwd_yz), ("skip", skip_in, skip),
        ("weight", weight, raw), ("fwd_x", fwd_x_in, fwd_x), ("inv_x", inv_x_in, inv_x),
        ("inv_y", inv_y_in, inv_y), ("inv_z", inv_z_in, inv_z), ("bias", bias_in, bias),
        ("head", head_in, head),
    )):
        loads[name] = pltpu.make_async_copy(src, dst, load_sem.at[k])

    barrier = pltpu.get_barrier_semaphore()

    def greet(to):
        pl.semaphore_signal(barrier, inc=1, device_id=(to, chan), device_id_type=MESH)

    each_slab(me, greet)
    for k in range(1, CHANS):
        pl.semaphore_signal(
            barrier, inc=1, device_id=(me, lax.rem(chan + k, CHANS)), device_id_type=MESH
        )
    for load in loads.values():
        load.start()
    pending = []
    for name in ("feats", "coords", "counts", "lift"):
        loads[name].wait()

    lane = iota((16, POINTS), 1)
    mask = jnp.where((lane & 15) == iota((16, POINTS), 0), 1.0, 0.0)
    pick = jnp.where((iota((SLABS, POINTS), 1) >> 4) == iota((SLABS, POINTS), 0), 1.0, 0.0).astype(BF16)
    embed = dot(lift[...], feats[...]).astype(BF16).astype(F32)
    spot = coords[...]
    cell = (spot >> 4).astype(F32)
    part = (spot & 15).astype(F32)
    rows = [embed[v : v + 1] for v in range(8)]
    rows += [cell[v : v + 1] for v in range(3)] + [part[v : v + 1] for v in range(3)]
    spread = [(row * mask).astype(BF16) for row in rows]
    spread += [jnp.zeros((32, POINTS), BF16)]
    sorted_ = dot_nt(pick, jnp.concatenate(spread, axis=0))
    wide = jnp.broadcast_to(counts[...].astype(F32), (SLABS, SLABS))
    here = jnp.sum(jnp.where(iota((SLABS, SLABS), 0) == iota((SLABS, SLABS), 1), wide, 0.0), axis=1, keepdims=True)
    live = (iota((SLABS, 128), 1) & 15).astype(F32) < here
    a_send[0:1, 0:1, :] = jnp.zeros((1, 1, 128), F32)
    a_send[0:1, 1:2, :] = jnp.full((1, 1, 128), -8.0, F32)
    a_send[1 : SLABS + 1, 0:1, :] = jnp.where(live, sorted_[:, :128], 0.0).reshape(SLABS, 1, 128)
    a_send[1 : SLABS + 1, 1:2, :] = sorted_[:, 128:].reshape(SLABS, 1, 128)

    pl.semaphore_wait(barrier, SLABS - 1 + CHANS - 1)
    exchange(
        a_send, a_recv, a_sem.at[0], a_sem.at[1], me, chan,
        lambda src, to: src.at[pl.ds(to, 2)],
    )
    a_recv[pl.ds(me, 1)] = a_send[pl.ds(me, 2)].reshape(1, 2, 2, 128)
    a_all = all_but_one(a_recv, a_sem.at[0], a_sem.at[1], me, chan)
    pending.append(a_all)
    a_all.wait_recv()

    low = iota((8, 128), 1) < 64
    for which in range(2):
        got = a_recv[:, 1 - which]
        t_ref[which] = jnp.concatenate(
            [got[:, 0:1, :].reshape(SLABS, 128), got[:, 1:2, :].reshape(SLABS, 128)], axis=0
        ).T
        for k in range(8):
            first = t_ref[which, pl.ds(k, 8, stride=16), :]
            second = t_ref[which, pl.ds(k + 8, 8, stride=16), :]
            values = jnp.where(low, first, pltpu.roll(second, 64, 1))
            places = jnp.where(low, pltpu.roll(first, 64, 1), second)
            lanes = pl.ds(k * 128, 128)
            points[which, 0:8, lanes] = values
            points[which, 8:11, lanes] = places[0:3] + (places[3:6] + 0.5) * 0.0625
    embeds[pl.ds(chan, 1)] = points[:, 0:8, :].reshape(1, 2, 8, POINTS)

    def share(k, owner, to):
        return pltpu.make_async_remote_copy(
            src_ref=points.at[:, 0:8],
            dst_ref=embeds.at[owner],
            send_sem=m_send.at[k],
            recv_sem=m_recv.at[k],
            device_id=(me, to),
            device_id_type=MESH,
        )

    for k in (1, 3, 2):
        share(k, chan, lax.rem(chan + k, CHANS)).start()
        pending.append(share(k, chan, chan))

    loads["fwd_yz"].wait()
    base = (me * 2).astype(F32)
    down = iota((128, POINTS), 0).astype(F32)

    def transform(which, lhs, rhs):
        lanes = slice(which * POINTS, (which + 1) * POINTS)
        real_lanes, imag_lanes = slice(0, POINTS), slice(POINTS, 2 * POINTS)
        hat_y[:, lanes] = hat(down, points[which, 9:10, :]).astype(BF16)
        hat_z[:, lanes] = hat(down, points[which, 10:11, :]).astype(BF16)
        line_y = dot(fwd_yz[0:128, :], hat_y[:, lanes])
        line_z = dot(fwd_yz[128:192, :], hat_z[:, lanes])
        local = points[which, 8:9, :] - base
        planes = 2 - which
        for plane in range(planes):
            near = hat(float(plane), local)
            along[plane : plane + 1, lanes] = near
            real = (line_y[0:64] * near).astype(BF16)
            imag = (line_y[64:128] * near).astype(BF16)
            top = slice(plane * 64, plane * 64 + 64)
            low = slice((planes + plane) * 64, (planes + plane) * 64 + 64)
            lhs[top, real_lanes] = real
            lhs[top, imag_lanes] = -imag
            lhs[low, real_lanes] = imag
            lhs[low, imag_lanes] = real
        for c in range(8):
            row = points[which, c : c + 1, :]
            rhs[c * 32 : c * 32 + 32, real_lanes] = (line_z[0:32] * row).astype(BF16)
            rhs[c * 32 : c * 32 + 32, imag_lanes] = (line_z[32:64] * row).astype(BF16)
        result = dot_nt(lhs[...], rhs[...])
        for part_ in range(2):
            for plane in range(planes):
                for half in range(2):
                    rows = pl.ds(half * 4 + plane * 2 + part_, 64, stride=8)
                    at = (part_ * planes + plane) * 64
                    piece = result[at : at + 64, half * 128 : half * 128 + 128]
                    stage[rows, :] = stage[rows, :] + piece if which else piece

    transform(0, lhs, rhs)
    transform(1, lhs_prior, rhs_prior)
    c_send[...] = stage[...].reshape(SLABS, 8, 128).astype(BF16)
    exchange(c_send, c_recv, c_sem.at[0], c_sem.at[1], me, chan)
    c_recv[pl.ds(me, 1)] = c_send[pl.ds(me, 1)]
    c_all = all_but_one(c_recv, c_sem.at[0], c_sem.at[1], me, chan)
    pending.append(c_all)

    loads["weight"].wait()

    def pack(step, carry):
        kind = step // 16
        rest = step % 16
        source = (rest // 4) * 8 + rest % 4
        one = raw[kind, source]
        two = raw[kind, source + 4]
        packed[kind, rest] = jnp.concatenate([one, two], axis=-1)
        return carry

    lax.fori_loop(0, 32, pack, 0)

    for k in range(1, CHANS):
        share(k, lax.rem(chan + CHANS - k, CHANS), chan).wait_recv()
    loads["skip"].wait()
    for which in range(2):
        packet[which] = dot(skip[...], embeds[:, which].reshape(32, POINTS).astype(BF16))
    loads["bias"].wait()

    def spread(row, plane, which):
        lanes = slice(which * POINTS, (which + 1) * POINTS)
        values = hat_y[:, lanes].astype(F32) * (row * along[plane : plane + 1, lanes])
        high = values.astype(BF16)
        return high, (values - high.astype(F32)).astype(BF16)

    def deposit_own(o, carry):
        row = packet[0, pl.ds(o, 1), :]
        pieces = [*spread(row, 0, 0), *spread(row, 1, 0)]
        sums_z = dot_nt(jnp.concatenate(pieces, axis=0), hat_z[:, 0:POINTS])
        skipped[o, :, 0:128] = sums_z[0:128] + sums_z[128:256] + bias[o]
        skipped[o, :, 128:256] = sums_z[256:384] + sums_z[384:512] + bias[o]
        return carry

    lax.fori_loop(0, DEPOSIT_C, deposit_own, 0)
    c_all.wait_recv()

    loads["fwd_x"].wait()
    modes = dot(fwd_x[...], c_recv[...].astype(F32).reshape(512, 128).astype(BF16))
    turned = jnp.concatenate([modes[0:128].T, modes[128:256].T], axis=0).astype(BF16)
    d_recv[pl.ds(chan, 1)] = turned.reshape(1, 256, 128)

    def gather(k, owner, to):
        return pltpu.make_async_remote_copy(
            src_ref=d_recv.at[owner],
            dst_ref=d_recv.at[owner],
            send_sem=d_send.at[k],
            recv_sem=d_rsem.at[k],
            device_id=(me, to),
            device_id_type=MESH,
        )

    for k in (1, 3, 2):
        gather(k, chan, lax.rem(chan + k, CHANS)).start()
        pending.append(gather(k, chan, chan))

    lax.fori_loop(DEPOSIT_C, DEPOSIT_D, deposit_own, 0)
    for k in (0, 1, 3, 2):
        owner = lax.rem(chan + CHANS - k, CHANS)
        if k:
            gather(k, owner, chan).wait_recv()
        def mix(o, carry, k=k, owner=owner):
            if k:
                real, imag = acc[0, o], acc[1, o]
            else:
                real = imag = jnp.zeros((MZ, 128), F32)
            for group in range(4):
                at = owner * 4 + group
                wr, wi = packed[0, at, o], packed[1, at, o]
                vr = d_recv[owner, group * 32 : group * 32 + 32, :].astype(F32)
                vi = d_recv[owner, 128 + group * 32 : 128 + group * 32 + 32, :].astype(F32)
                real = real + (wr * vr - wi * vi)
                imag = imag + (wr * vi + wi * vr)
            acc[0, o] = real
            acc[1, o] = imag
            return carry

        lax.fori_loop(0, 8, mix, 0)
    low = iota((MZ, 128), 1) < 64
    mixed = []
    for o in range(8):
        real, imag = acc[0, o], acc[1, o]
        real = real + pltpu.roll(real, 64, 1)
        imag = imag + pltpu.roll(imag, 64, 1)
        mixed.append(jnp.where(low, real, imag).astype(BF16))
    mixed = jnp.concatenate(
        [jnp.concatenate(mixed[0:4], axis=0), jnp.concatenate(mixed[4:8], axis=0)], axis=1
    )
    loads["inv_x"].wait()
    e_send[...] = dot_nt(inv_x[...], mixed).reshape(SLABS, 8, 128).astype(BF16)
    exchange(e_send, e_recv, e_sem.at[0], e_sem.at[1], me, chan)
    e_recv[pl.ds(me, 1)] = e_send[pl.ds(me, 1)]
    e_all = all_but_one(e_recv, e_sem.at[0], e_sem.at[1], me, chan)
    pending.append(e_all)

    lax.fori_loop(DEPOSIT_D, 8, deposit_own, 0)

    def deposit_prior(o, carry):
        high, rest = spread(packet[1, pl.ds(o, 1), :], 0, 1)
        sums_z = dot_nt(jnp.concatenate([high, rest], axis=0), hat_z[:, POINTS : 2 * POINTS])
        skipped[o, :, 0:128] = skipped[o, :, 0:128] + (sums_z[0:128] + sums_z[128:256])
        return carry

    lax.fori_loop(0, 8, deposit_prior, 0)
    e_all.wait_recv()

    loads["inv_y"].wait()
    loads["inv_z"].wait()
    lines = dot(inv_y[...], e_recv[...].astype(F32).reshape(512, 128).astype(BF16)).astype(BF16)
    both = [
        jnp.concatenate([lines[at : at + 128], lines[at + 128 : at + 256]], axis=1)
        for at in range(0, 1024, 256)
    ]
    result = dot(jnp.concatenate(both, axis=0), inv_z[...])
    for block in range(4):
        half, plane = block // 2, block % 2
        for group in range(4):
            spectral[half * 4 + group, :, plane * 128 : plane * 128 + 128] = result[
                block * 128 : block * 128 + 128, group * 128 : group * 128 + 128
            ]

    loads["head"].wait()
    heading = 0.5 * head[...].astype(F32)
    shape = (32, 256)
    scale = math.sqrt(2.0 / math.pi)

    def activate(step, carry):
        at = pl.ds(step * 32, 32)
        fields = [jnp.zeros(shape, F32) for _ in range(4)]
        for o in range(8):
            x = spectral[o, at, :] + skipped[o, at, :]
            h = x + x * jnp.tanh(x * (scale + (scale * 0.044715) * (x * x)))
            for n in range(4):
                fields[n] = fields[n] + jnp.broadcast_to(heading[n : n + 1, o : o + 1], shape) * h
        for n in range(4):
            high = fields[n].astype(BF16)
            rest = (fields[n] - high.astype(F32)).astype(BF16)
            for plane in range(2):
                z = slice(plane * 128, plane * 128 + 128)
                hn[plane, n, at, 0:128] = high[:, z]
                hn[plane, n, at, 128:256] = rest[:, z]
        return carry

    lax.fori_loop(0, 4, activate, 0)

    fields = hn[...].reshape(1024, 256)
    for block in range(8):
        lanes = pl.ds(block * 256, 256)
        planes = 2 if block < 4 else 1
        grid_z = hat_z[:, lanes]
        along_z = dot(fields[0 : planes * 512], jnp.concatenate([grid_z, grid_z], axis=0))
        grid_y = hat_y[:, lanes].astype(F32)
        for n in range(4):
            sampled = jnp.zeros((1, 256), F32)
            for plane in range(planes):
                at = plane * 512 + n * 128
                line = jnp.sum(along_z[at : at + 128] * grid_y, axis=0, keepdims=True)
                sampled = sampled + line * along[plane : plane + 1, lanes]
            which = block // 4
            heads[which * 4 + n : which * 4 + n + 1, pl.ds((block % 4) * 256, 256)] = sampled
    for k in range(8):
        piece = heads[:, k * 128 : k * 128 + 128]
        back[pl.ds(k, 8, stride=16), :] = piece
        back[pl.ds(k + 8, 8, stride=16), :] = pltpu.roll(piece, 64, 1)
    h_send[...] = back[...].T[0:SLABS].reshape(SLABS, 1, 128)
    exchange(h_send, h_recv, h_sem.at[0], h_sem.at[1], me, chan)
    h_recv[pl.ds(me, 1)] = h_send[pl.ds(me, 1)]
    h_all = all_but_one(h_recv, h_sem.at[0], h_sem.at[1], me, chan)
    pending.append(h_all)
    h_all.wait_recv()

    home = h_recv[...].reshape(SLABS, 128)
    home = home + pltpu.roll(pltpu.roll(home, SLABS - 1, 0), 64, 1)
    narrow = iota((32, 128), 1) < 64
    sums[pl.ds(chan, 1)] = jnp.where(narrow, home[0:32], pltpu.roll(home[32:64], 64, 1)).reshape(1, 32, 128)

    def total(k, owner, to):
        return pltpu.make_async_remote_copy(
            src_ref=sums.at[owner],
            dst_ref=sums.at[owner],
            send_sem=g_send.at[k],
            recv_sem=g_recv.at[k],
            device_id=(me, to),
            device_id_type=MESH,
        )

    for k in (1, 3, 2):
        total(k, chan, lax.rem(chan + k, CHANS)).start()
        pending.append(total(k, chan, chan))
    pick2 = jnp.where((iota((SLABS, POINTS), 1) >> 4) == iota((SLABS, POINTS), 0), 1.0, 0.0).astype(BF16)
    cover = dot(jnp.broadcast_to(counts[...].astype(F32), (8, SLABS)).astype(BF16), pick2)
    alive = (iota((4, POINTS), 1) & 15).astype(F32) < cover[0:4]
    for k in range(1, CHANS):
        total(k, lax.rem(chan + CHANS - k, CHANS), chan).wait_recv()
    home = sums[0] + sums[1] + sums[2] + sums[3]
    home = jnp.concatenate([home, pltpu.roll(home, 64, 1)], axis=0)
    turned = jnp.concatenate([home, jnp.zeros_like(home)], axis=0).T[0:SLABS, 0:SLABS]
    top = turned.astype(BF16)
    rest = turned - top.astype(F32)
    middle = rest.astype(BF16)
    bottom = (rest - middle.astype(F32)).astype(BF16)
    laid = dot(top, pick2) + dot(middle, pick2) + dot(bottom, pick2)
    for n in range(4):
        line = jnp.sum(laid[n * 16 : n * 16 + 16] * mask, axis=0, keepdims=True)
        out[n : n + 1, :] = jnp.where(alive[n : n + 1], line, 0.0)
    out[4:8, :] = jnp.where(alive, 1.0, 0.0)

    for copy in pending:
        copy.wait_send()


def local(
    point_feats, cell_coords, send_counts, lift_weight, spec_weight,
    skip_weight, spec_bias, out_weight, out_bias,
):
    weight = jnp.swapaxes(spec_weight, 4, 5).reshape(2, 32, 8, MZ, 64)
    vmem = pl.BlockSpec(memory_space=pltpu.VMEM)
    hbm = pl.BlockSpec(memory_space=pltpu.HBM)
    dma = pltpu.SemaphoreType.DMA
    scratch = [
        pltpu.VMEM((32, POINTS), BF16),
        pltpu.VMEM((3, POINTS), jnp.int32),
        pltpu.VMEM((1, SLABS), jnp.int32),
        pltpu.VMEM((8, 32), BF16),
        pltpu.VMEM((8, 32), BF16),
        pltpu.SMEM((8,), F32),
        pltpu.VMEM((4, 8), BF16),
        pltpu.VMEM((192, 128), BF16),
        pltpu.VMEM((256, 512), BF16),
        pltpu.VMEM((512, 256), BF16),
        pltpu.VMEM((1024, 512), BF16),
        pltpu.VMEM((256, 512), BF16),
        pltpu.VMEM((SLABS + 1, 2, 128), F32),
        pltpu.VMEM((SLABS, 2, 2, 128), F32),
        pltpu.VMEM((2, 128, 128), F32),
        pltpu.VMEM((2, 16, POINTS), F32),
        pltpu.VMEM((CHANS, 2, 8, POINTS), F32),
        pltpu.VMEM((2, 8, POINTS), F32),
        pltpu.VMEM((8, 2 * POINTS), F32),
        pltpu.VMEM((128, 2 * POINTS), BF16),
        pltpu.VMEM((128, 2 * POINTS), BF16),
        pltpu.VMEM((256, 2 * POINTS), BF16),
        pltpu.VMEM((256, 2 * POINTS), BF16),
        pltpu.VMEM((128, 2 * POINTS), BF16),
        pltpu.VMEM((256, 2 * POINTS), BF16),
        pltpu.VMEM((512, 128), F32),
        pltpu.VMEM((SLABS, 8, 128), BF16),
        pltpu.VMEM((SLABS, 8, 128), BF16),
        pltpu.VMEM((2, 32, 8, MZ, 64), F32),
        pltpu.VMEM((2, 16, 8, MZ, 128), F32),
        pltpu.VMEM((CHANS, 256, 128), BF16),
        pltpu.VMEM((2, 8, MZ, 128), F32),
        pltpu.VMEM((SLABS, 8, 128), BF16),
        pltpu.VMEM((SLABS, 8, 128), BF16),
        pltpu.VMEM((8, 128, 256), F32),
        pltpu.VMEM((8, 128, 256), F32),
        pltpu.VMEM((2, 4, 128, 256), BF16),
        pltpu.VMEM((8, POINTS), F32),
        pltpu.VMEM((128, 128), F32),
        pltpu.VMEM((SLABS, 1, 128), F32),
        pltpu.VMEM((SLABS, 1, 128), F32),
        pltpu.VMEM((CHANS, 32, 128), F32),
        dma((13,)),
        dma((2,)),
        dma((2,)),
        dma((2,)),
        dma((2,)),
        dma((CHANS,)),
        dma((CHANS,)),
        dma((CHANS,)),
        dma((CHANS,)),
        dma((CHANS,)),
        dma((CHANS,)),
    ]
    result = pl.pallas_call(
        kernel,
        out_shape=jax.ShapeDtypeStruct((8, POINTS), F32),
        in_specs=[hbm] * 13,
        out_specs=vmem,
        scratch_shapes=scratch,
        compiler_params=pltpu.CompilerParams(
            collective_id=0, has_side_effects=True, vmem_limit_bytes=60 * 1024 * 1024
        ),
    )(
        point_feats, cell_coords, send_counts, lift_weight.T, weight,
        skip_weight.T, spec_bias, out_weight.T, *(jnp.asarray(t) for t in tables()),
    )
    return result[0:4] + out_bias[:, None] * result[4:8]


def solution(mesh):
    in_specs = (
        P(None, "slab"),
        P(None, "slab"),
        P("slab", None),
        P(None, "chan"),
        P(None, None, "chan", "slab", None, None),
        P(None, "chan"),
        P("chan"),
        P("chan", None),
        P(),
    )
    out_specs = P(None, "slab")
    return jax.shard_map(local, mesh=mesh, in_specs=in_specs, out_specs=out_specs, check_vma=False)
```
